512 devices in a mesh: rep: 32 (over z_lo, y, core), fsdp: 16 (over z_hi, x).
Axes of the slice: x: 4, y: 4, z: 16 (z_hi: 4, z_lo: 4; z = z_hi * 4 + z_lo), core: 2. Of those that a mesh axis runs over, the one named last changes fastest.
Arguments:
- inputs: bfloat16 [2, 65536, 4096], P(None, ('rep', 'fsdp')), may hold values from -3000 to 3000
- cotangent: bfloat16 [2, 65536, 512], P(None, ('rep', 'fsdp')), may hold values from -6 to 6
- weight: float32 [32, 4096, 512], P('rep', 'fsdp'), may hold values from -6 to 6
- norm_gain: float32 [32, 4096], P('rep', 'fsdp'), may hold values from 0.5 to 1.5
- adam_first: bfloat16 [32, 4096, 512], P('rep', 'fsdp'), may hold values from -0.00059890747 to 0.00059890747
- adam_second: bfloat16 [32, 4096, 512], P('rep', 'fsdp'), may hold values from 9.95351e-09 to 9.9651515e-08
- gain_first: float32 [32, 4096], P('rep', 'fsdp'), may hold values from -0.006 to 0.006
- gain_second: float32 [32, 4096], P('rep', 'fsdp'), may hold values from 1e-05 to 0.0001
- anchor_weight: float32 [4096, 512], P('fsdp'), may hold values from -6 to 6
- anchor_gain: float32 [4096], P('fsdp'), may hold values from 0.5 to 1.5
- outer_weight: float32 [4096, 512], P('fsdp'), may hold values from -3 to 3
- outer_gain: float32 [4096], P('fsdp'), may hold values from -0.3 to 0.3
Outputs:
- merged_weight: float32 [32, 4096, 512], P('rep', 'fsdp')
- merged_gain: float32 [32, 4096], P('rep', 'fsdp')
The draws below stay inside these ranges and needn't reach their ends.
All inputs are finite; a program needn't handle non-finite values.
Results may differ from the reference program's by a relative error of at most 0.007.
Values may be sent and summed in bfloat16 or wider, within the bound.
A program may use at most 64 MiB of HBM per device.

```python
import math
import jax
import jax.numpy as jnp
from jax import lax

D = 4096
KW = 512
TOK_DEV = 128
INNER = 2
TOKENS = 65536
N_REP = 32
N_FSDP = 16


def draw_inputs(key, part):
    key = jax.random.fold_in(key, 11)
    key_noise = jax.random.fold_in(key, 0)
    key_column = jax.random.fold_in(key, 1)
    key_row = jax.random.fold_in(key, 3)
    column = jnp.exp(jax.random.uniform(key_column, (D,), jnp.float32, 0.0, math.log(10.0)))
    row_scale = jnp.exp(jax.random.uniform(key_row, (INNER, TOKENS, 1), jnp.float32, 0.0, math.log(10.0)))
    position = jnp.arange(D, dtype=jnp.float32) / D
    noise_part = jnp.clip(jax.random.normal(key_noise, (INNER, TOKENS, D), jnp.float32), -4.0, 4.0)
    values = noise_part * jnp.exp(position * math.log(3.0))
    return (values * column[None, None, :] * row_scale).astype(jnp.bfloat16)


def level_of(stream_key, shape, shards, low, top_value):
    factor_of, own = 1.0, jax.random.fold_in(stream_key, 6)
    for dim, shards_of in shards:
        steps = jnp.exp(jax.random.uniform(jax.random.fold_in(own, dim), (shards_of,), jnp.float32, low / len(shards), top_value / len(shards)))
        factor_of = factor_of * jnp.repeat(steps, shape[dim] // shards_of).reshape([-1 if axis == dim else 1 for axis in range(len(shape))])
    return factor_of


def scatter_about(stream_key, shape, width, most, cuts=(), held_as=jnp.bfloat16):
    array = width * jax.random.normal(stream_key, shape, jnp.float32)
    if cuts:
        array = array * level_of(stream_key, shape, cuts, -0.22, 0.18)
    return jnp.clip(array, -most, most).astype(held_as)


def setup_inputs(seed: int = 0) -> dict:
    key_list = jax.random.split(jax.random.key(seed), 13)
    inputs = draw_inputs(jax.random.fold_in(key_list[12], 71), 0)
    cotangent = scatter_about(key_list[1], (INNER, TOKENS, KW), 1.0, 6.0, ((1, 512),))
    weight = scatter_about(key_list[2], (N_REP, D, KW), 1.0, 6.0, ((0, 32), (1, 16)), jnp.float32)
    norm_gain = jnp.clip(1.0 + 0.1 * jax.random.normal(key_list[3], (N_REP, D), jnp.float32), 0.5, 1.5)
    adam_first = scatter_about(key_list[4], (N_REP, D, KW), 0.0001, 0.00059890747, ((0, 32), (1, 16)))
    adam_second = jnp.clip(jnp.exp(math.log(9.96515154838562e-08) - 2.303754 * jax.random.uniform(key_list[5], (N_REP, D, KW), jnp.float32) ** level_of(key_list[5], (N_REP, D, KW), ((0, 32), (1, 16)), -0.2, 0.2)), 9.953510016202927e-09, 9.96515154838562e-08).astype(jnp.bfloat16)
    gain_first = scatter_about(key_list[6], (N_REP, D), 0.001, 0.006, ((0, 32), (1, 16)), jnp.float32)
    gain_second = jnp.clip(jnp.exp(math.log(0.0001) - 2.3025851 * jax.random.uniform(key_list[7], (N_REP, D), jnp.float32) ** level_of(key_list[7], (N_REP, D), ((0, 32), (1, 16)), -0.2, 0.2)), 9.999999747378752e-06, 0.0001)
    anchor_weight = scatter_about(key_list[8], (D, KW), 1.0, 6.0, ((0, 16),), jnp.float32)
    anchor_gain = jnp.clip(1.0 + 0.1 * jax.random.normal(key_list[9], (D,), jnp.float32), 0.5, 1.5)
    outer_weight = scatter_about(key_list[10], (D, KW), 0.5, 3.0, ((0, 16),), jnp.float32)
    outer_gain = scatter_about(key_list[11], (D,), 0.05, 0.3, ((0, 16),), jnp.float32)
    return dict(inputs=inputs, cotangent=cotangent, weight=weight, norm_gain=norm_gain, adam_first=adam_first, adam_second=adam_second, gain_first=gain_first, gain_second=gain_second, anchor_weight=anchor_weight, anchor_gain=anchor_gain, outer_weight=outer_weight, outer_gain=outer_gain)


BETA_ONE = 0.9
BETA_TWO = 0.999
EPS_ADAM = 1e-08
RATE = 0.3
DECAY = 0.1
EPS_NORM = 1e-05
OUTER_RATE = 0.7
MOMENTUM = 0.9
MIXING = 0.5

def inverse_rms(values):
    widened = values.astype(jnp.float32)
    return lax.rsqrt(lax.optimization_barrier(jnp.mean(widened * widened, axis=-1)) + EPS_NORM)

def adam_update(current, gradient, moment_one, moment_two, decay_rate):
    moment_one = BETA_ONE * moment_one + (1.0 - BETA_ONE) * gradient
    moment_two = BETA_TWO * moment_two + (1.0 - BETA_TWO) * gradient * gradient
    current = current - RATE * (moment_one / (jnp.sqrt(moment_two) + EPS_ADAM) + decay_rate * current)
    return (current, moment_one, moment_two)

def outer_step(anchor, momentum, mean_delta):
    velocity = MOMENTUM * momentum + mean_delta
    return anchor - OUTER_RATE * (mean_delta + MOMENTUM * velocity)

def replica_window(batch, cotangents, current, gain_now, moment_one, moment_two, gain_one, gain_two):
    scales = inverse_rms(batch)
    for inner_step in range(INNER):
        normed = batch[inner_step].astype(jnp.float32) * scales[inner_step][:, None]
        hidden = (normed * gain_now[None, :]).astype(jnp.bfloat16)
        grad_weight = lax.dot_general(hidden, cotangents[inner_step], (((0,), (0,)), ((), ())), preferred_element_type=jnp.float32)
        weight_low = current.astype(jnp.bfloat16)
        back_grad = lax.dot_general(cotangents[inner_step], weight_low, (((1,), (1,)), ((), ())), preferred_element_type=jnp.float32)
        grad_gain = lax.optimization_barrier(jnp.sum(normed * back_grad, axis=0))
        squares = jnp.sum(grad_weight * grad_weight) + jnp.sum(grad_gain * grad_gain)
        factor = jnp.minimum(1.0, 1.0 / (jnp.sqrt(squares) + 1e-06))
        current, moment_one, moment_two = adam_update(current, factor * grad_weight, moment_one, moment_two, DECAY)
        gain_now, gain_one, gain_two = adam_update(gain_now, factor * grad_gain, gain_one, gain_two, 0.0)
    return (current, gain_now)

def reference(inputs, cotangent, weight, norm_gain, adam_first, adam_second, gain_first, gain_second, anchor_weight, anchor_gain, outer_weight, outer_gain):
    sum_weight = lax.optimization_barrier(jnp.sum(anchor_weight[None, :, :] - weight, axis=0))
    sum_gain = lax.optimization_barrier(jnp.sum(anchor_gain[None, :] - norm_gain, axis=0))
    new_weight = outer_step(anchor_weight, outer_weight, sum_weight / N_REP)
    new_gain = outer_step(anchor_gain, outer_gain, sum_gain / N_REP)
    replica_rows = TOK_DEV * N_FSDP

    def per_replica(replica):
        offset = (replica * replica_rows).astype(jnp.int32)
        batch = lax.dynamic_slice_in_dim(inputs, offset, replica_rows, 1)
        cotangents = lax.dynamic_slice_in_dim(cotangent, offset, replica_rows, 1)
        return replica_window(batch, cotangents, weight[replica], norm_gain[replica], adam_first[replica].astype(jnp.float32), adam_second[replica].astype(jnp.float32), gain_first[replica], gain_second[replica])
    finals, gains = lax.map(per_replica, jnp.arange(N_REP, dtype=jnp.int32))
    merged_weight = MIXING * finals + (1.0 - MIXING) * new_weight[None, :, :]
    merged_gain = MIXING * gains + (1.0 - MIXING) * new_gain[None, :]
    return (merged_weight, merged_gain)
```

```python
import jax
import jax.numpy as jnp
from jax import lax
from jax.experimental import pallas as pl
from jax.experimental.pallas import tpu as pltpu
from jax.sharding import PartitionSpec as P

BETA_ONE = 0.9
BETA_TWO = 0.999
EPS_ADAM = 1e-08
RATE = 0.3
DECAY = 0.1
EPS_NORM = 1e-05
OUTER_RATE = 0.7
MOMENTUM = 0.9
MIXING = 0.5

INNER = 2
NX = 4
NZ = 4
NF = NX * NZ
TOK = 128
ROWS = 256
HALF = ROWS // 2
D = ROWS * NF
KW = 512
ORDER = (2, 1, 3, 0)

MESH = pl.DeviceIdType.MESH


def flip(value, bits):
    if bits == 0:
        return value
    if bits == 1:
        return value + 1 - 2 * (value % 2)
    if bits == 2:
        return (value + 2) % 4
    return 3 - value


def adam_update(current, gradient, moment_one, moment_two, decay_rate):
    moment_one = BETA_ONE * moment_one + (1.0 - BETA_ONE) * gradient
    moment_two = BETA_TWO * moment_two + (1.0 - BETA_TWO) * gradient * gradient
    current = current - RATE * (
        moment_one / (jnp.sqrt(moment_two) + EPS_ADAM) + decay_rate * current
    )
    return (current, moment_one, moment_two)


def outer_step(anchor, momentum, mean_delta):
    velocity = MOMENTUM * momentum + mean_delta
    return anchor - OUTER_RATE * (mean_delta + MOMENTUM * velocity)


def kernel(
    inputs,
    cotangent,
    weight,
    adam_first,
    adam_second,
    gains,
    out_weight,
    out_gain,
    xin,
    cin,
    win,
    m_one,
    m_two,
    columns,
    scaled,
    grads,
    keep,
    z_out,
    z_in,
    norms,
    local_sem,
    x_send,
    x_recv,
    c_send,
    c_recv,
    z_send,
    z_recv,
    q_send,
    q_recv,
):
    me = lax.axis_index("fsdp")
    my_z = me // NX
    my_x = me % NX

    def at(z, x):
        return {"fsdp": z * NX + x}

    loads = []
    for place, (source, target) in enumerate(
        (
            (inputs.at[0], xin.at[0]),
            (cotangent, cin),
            (inputs.at[1], xin.at[1]),
            (weight, win),
            (adam_first, m_one),
            (adam_second, m_two),
        )
    ):
        copy = pltpu.make_async_copy(source, target, local_sem.at[place])
        copy.start()
        loads.append(copy)

    def column(j, i):
        owner = flip(my_z, j) * NX + flip(my_x, i)
        return pl.ds(pl.multiple_of(owner * ROWS, ROWS), ROWS)

    own_copies = {}
    place = len(loads)
    for s in range(INNER):
        for j in ORDER:
            copy = pltpu.make_async_copy(
                inputs.at[s, :, column(j, 0)],
                columns.at[s, j, pl.ds(0, TOK)],
                local_sem.at[place],
            )
            copy.start()
            own_copies[s, j] = copy
            place += 1

    barrier = pltpu.get_barrier_semaphore()
    for k in range(1, NF):
        pl.semaphore_signal(
            barrier, inc=1, device_id={"fsdp": (me + k) % NF}, device_id_type=MESH
        )
    pl.semaphore_wait(barrier, NF - 1)

    sends = []

    def send(source, target, send_sem, recv_sem, device):
        copy = pltpu.make_async_remote_copy(
            src_ref=source,
            dst_ref=target,
            send_sem=send_sem,
            recv_sem=recv_sem,
            device_id=device,
            device_id_type=MESH,
        )
        copy.start()
        sends.append(copy)
        return copy

    x_copies = {}
    c_copies = {}
    z_copies = {}
    q_copies = {}

    def send_columns(s, j):
        x_copies[s, j] = [
            send(
                inputs.at[s, :, column(j, i)],
                columns.at[s, j, pl.ds(i * TOK, TOK)],
                x_send.at[s, j, i - 1],
                x_recv.at[s, j, i - 1],
                at(my_z, flip(my_x, i)),
            )
            for i in (1, 3, 2)
        ]

    def send_scaled(s):
        values = xin[s].astype(jnp.float32)
        mean = jnp.mean(values * values, axis=-1, keepdims=True)
        scale = lax.rsqrt(mean + EPS_NORM)
        scaled[s, pl.ds(0, TOK), :] = (cin[s].astype(jnp.float32) * scale).astype(
            jnp.bfloat16
        )
        c_copies[s] = [
            send(
                scaled.at[s, pl.ds(0, TOK)],
                scaled.at[s, pl.ds(i * TOK, TOK)],
                c_send.at[s, i - 1],
                c_recv.at[s, i - 1],
                at(my_z, flip(my_x, i)),
            )
            for i in (1, 3, 2)
        ]

    def send_rows(s, slot, j):
        z_copies[s, slot] = send(
            z_out.at[s, slot],
            z_in.at[s, slot],
            z_send.at[s, slot],
            z_recv.at[s, slot],
            at(flip(my_z, j), my_x),
        )

    chunks = [(s, j) for s in range(INNER) for j in ORDER]
    send_columns(*chunks[0])
    loads[0].wait()
    loads[1].wait()
    send_scaled(0)
    send_columns(*chunks[1])
    loads[2].wait()

    low = pl.ds(0, HALF)
    high = pl.ds(HALF, HALF)

    def product(number):
        s, j = chunks[number]
        own_copies[s, j].wait()
        for copy in x_copies[s, j]:
            copy.wait_recv()
        if j == ORDER[0]:
            for copy in c_copies[s]:
                copy.wait_recv()
        if number + 2 < len(chunks):
            send_columns(*chunks[number + 2])
            if number == 1:
                send_scaled(1)
        block = lax.dot_general(
            columns[s, j],
            scaled[s],
            (((0,), (0,)), ((), ())),
            preferred_element_type=jnp.float32,
        )
        if j == 2:
            z_out[s, 0] = block[:HALF].astype(jnp.bfloat16)
            send_rows(s, 0, 1)
            z_out[s, 1] = block[HALF:].astype(jnp.bfloat16)
            send_rows(s, 1, 3)
        elif j == 1:
            z_out[s, 2] = block[:HALF].astype(jnp.bfloat16)
            send_rows(s, 2, 1)
            keep[s, 1] = block[HALF:]
        elif j == 3:
            z_out[s, 3] = block[HALF:].astype(jnp.bfloat16)
            send_rows(s, 3, 3)
            keep[s, 0] = block[:HALF]
        else:
            grads[s] = block

    def forward(s):
        z_copies[s, 0].wait_recv()
        z_out[s, 4] = (keep[s, 0] + z_in[s, 0].astype(jnp.float32)).astype(jnp.bfloat16)
        send_rows(s, 4, 3)
        z_copies[s, 1].wait_recv()
        z_out[s, 5] = (keep[s, 1] + z_in[s, 1].astype(jnp.float32)).astype(jnp.bfloat16)
        send_rows(s, 5, 1)

    def reduce_rows(s):
        for slot in (2, 3, 4, 5):
            z_copies[s, slot].wait_recv()
        grads[s, low] = grads[s, low] + (
            z_in[s, 2].astype(jnp.float32) + z_in[s, 4].astype(jnp.float32)
        )
        grads[s, high] = grads[s, high] + (
            z_in[s, 3].astype(jnp.float32) + z_in[s, 5].astype(jnp.float32)
        )

    def update(s, current, gain, moments, gain_moments):
        product_sum = grads[s]
        low_weight = current.astype(jnp.bfloat16).astype(jnp.float32)
        grad_gain = jnp.sum(product_sum * low_weight, axis=1, keepdims=True)
        grad_weight = product_sum * gain
        squares = grad_weight * grad_weight
        folded = squares[:, 0:128] + squares[:, 128:256] + squares[:, 256:384] + squares[:, 384:512]
        lane = lax.broadcasted_iota(jnp.int32, (ROWS, 128), 1)
        folded = folded + jnp.where(lane == 0, grad_gain * grad_gain, 0.0)
        norms[s, 0] = jnp.sum(folded.reshape(ROWS // 8, 8, 128), axis=0)
        q_copies[s] = [
            send(
                norms.at[s, 0],
                norms.at[s, k],
                q_send.at[s, k - 1],
                q_recv.at[s, k - 1],
                {"fsdp": (me + k) % NF},
            )
            for k in range(1, NF)
        ]
        for copy in q_copies[s]:
            copy.wait_recv()
        total = jnp.sum(jnp.sum(norms[s], axis=0), keepdims=True)
        factor = jnp.minimum(1.0, 1.0 / (jnp.sqrt(total) + 1e-06))
        current, one, two = adam_update(
            current, factor * grad_weight, moments[0], moments[1], DECAY
        )
        gain, gain_one, gain_two = adam_update(
            gain, factor * grad_gain, gain_moments[0], gain_moments[1], 0.0
        )
        return current, gain, (one, two), (gain_one, gain_two)

    for number in range(len(ORDER)):
        product(number)
    forward(0)
    for number in range(len(ORDER), 2 * len(ORDER)):
        product(number)
    for copy in loads[3:]:
        copy.wait()
    turned = jnp.transpose(gains[...])
    reduce_rows(0)
    current, gain, moments, gain_moments = update(
        0,
        win[...],
        turned[:, 0:1],
        (m_one[...].astype(jnp.float32), m_two[...].astype(jnp.float32)),
        (turned[:, 1:2], turned[:, 2:3]),
    )
    forward(1)
    reduce_rows(1)
    current, gain, _, _ = update(1, current, gain, moments, gain_moments)
    out_weight[...] = current
    out_gain[...] = jnp.transpose(jnp.broadcast_to(gain, (ROWS, 8)))
    for copy in sends:
        copy.wait_send()


def window(inputs, cotangent, weight, adam_first, adam_second, gains):
    anywhere = pl.BlockSpec(memory_space=pl.ANY)
    vmem = pl.BlockSpec(memory_space=pltpu.VMEM)
    dma = pltpu.SemaphoreType.DMA
    f32, bf16 = jnp.float32, jnp.bfloat16
    return pl.pallas_call(
        kernel,
        out_shape=(
            jax.ShapeDtypeStruct((ROWS, KW), f32),
            jax.ShapeDtypeStruct((8, ROWS), f32),
        ),
        in_specs=[anywhere] * 5 + [vmem],
        out_specs=(vmem, vmem),
        scratch_shapes=[
            pltpu.VMEM((INNER, TOK, D), bf16),
            pltpu.VMEM((INNER, TOK, KW), bf16),
            pltpu.VMEM((ROWS, KW), f32),
            pltpu.VMEM((ROWS, KW), bf16),
            pltpu.VMEM((ROWS, KW), bf16),
            pltpu.VMEM((INNER, NZ, NX * TOK, ROWS), bf16),
            pltpu.VMEM((INNER, NX * TOK, KW), bf16),
            pltpu.VMEM((INNER, ROWS, KW), f32),
            pltpu.VMEM((INNER, 2, HALF, KW), f32),
            pltpu.VMEM((INNER, 6, HALF, KW), bf16),
            pltpu.VMEM((INNER, 6, HALF, KW), bf16),
            pltpu.VMEM((INNER, NF, 8, 128), f32),
            dma((6 + INNER * NZ,)),
            dma((INNER, NZ, NX - 1)),
            dma((INNER, NZ, NX - 1)),
            dma((INNER, NX - 1)),
            dma((INNER, NX - 1)),
            dma((INNER, 6)),
            dma((INNER, 6)),
            dma((INNER, NF - 1)),
            dma((INNER, NF - 1)),
        ],
        compiler_params=pltpu.CompilerParams(
            collective_id=0, has_side_effects=True, vmem_limit_bytes=40 * 1024 * 1024
        ),
        cost_estimate=pl.CostEstimate(
            flops=4 * INNER * NX * TOK * NZ * ROWS * KW,
            bytes_accessed=8 * 1024 * 1024,
            transcendentals=0,
        ),
        name="inner_window",
    )(inputs, cotangent, weight, adam_first, adam_second, gains)


def on_device(
    inputs,
    cotangent,
    weight,
    norm_gain,
    adam_first,
    adam_second,
    gain_first,
    gain_second,
    anchor_weight,
    anchor_gain,
    outer_weight,
    outer_gain,
):
    replicas = lax.axis_size("rep")
    sum_weight, sum_gain = lax.psum(
        (anchor_weight - weight[0], anchor_gain - norm_gain[0]), "rep"
    )
    gains = jnp.concatenate(
        (norm_gain, gain_first, gain_second, jnp.zeros((5, ROWS), jnp.float32)), axis=0
    )
    current, gain_now = window(
        inputs, cotangent, weight[0], adam_first[0], adam_second[0], gains
    )
    new_weight = outer_step(anchor_weight, outer_weight, sum_weight / replicas)
    new_gain = outer_step(anchor_gain, outer_gain, sum_gain / replicas)
    merged_weight = MIXING * current + (1.0 - MIXING) * new_weight
    merged_gain = MIXING * gain_now[0] + (1.0 - MIXING) * new_gain
    return (merged_weight[None], merged_gain[None])


def solution(mesh):
    return jax.shard_map(
        on_device,
        mesh=mesh,
        in_specs=(
            P(None, ("rep", "fsdp"), None),
            P(None, ("rep", "fsdp"), None),
            P("rep", "fsdp", None),
            P("rep", "fsdp"),
            P("rep", "fsdp", None),
            P("rep", "fsdp", None),
            P("rep", "fsdp"),
            P("rep", "fsdp"),
            P("fsdp", None),
            P("fsdp"),
            P("fsdp", None),
            P("fsdp"),
        ),
        out_specs=(P("rep", "fsdp", None), P("rep", "fsdp")),
        check_vma=False,
    )
```

```python
import jax
import jax.numpy as jnp
from jax import lax
from jax.experimental import pallas as pl
from jax.experimental.pallas import tpu as pltpu
from jax.sharding import PartitionSpec as P

BETA_ONE = 0.9
BETA_TWO = 0.999
EPS_ADAM = 1e-08
RATE = 0.3
DECAY = 0.1
EPS_NORM = 1e-05
OUTER_RATE = 0.7
MOMENTUM = 0.9
MIXING = 0.5

INNER = 2
NX = 4
NZ = 4
NF = NX * NZ
TOK = 128
ROWS = 256
HALF = ROWS // 2
D = ROWS * NF
KW = 512
NP = 8
NL = 4
PART = ROWS // NP
SUB = PART // NL
ORDER = (2, 1, 3, 0)

MESH = pl.DeviceIdType.MESH


def flip(value, bits):
    if bits == 0:
        return value
    if bits == 1:
        return value + 1 - 2 * (value % 2)
    if bits == 2:
        return (value + 2) % 4
    return 3 - value


def adam_update(current, gradient, moment_one, moment_two, decay_rate):
    moment_one = BETA_ONE * moment_one + (1.0 - BETA_ONE) * gradient
    moment_two = BETA_TWO * moment_two + (1.0 - BETA_TWO) * gradient * gradient
    current = current - RATE * (
        moment_one / (jnp.sqrt(moment_two) + EPS_ADAM) + decay_rate * current
    )
    return (current, moment_one, moment_two)


def outer_step(anchor, momentum, mean_delta):
    velocity = MOMENTUM * momentum + mean_delta
    return anchor - OUTER_RATE * (mean_delta + MOMENTUM * velocity)


def kernel(
    inputs,
    cotangent,
    weight,
    adam_first,
    adam_second,
    anchor_weight,
    outer_weight,
    gains,
    out_weight,
    out_gain,
    xin,
    cin,
    win,
    m_one,
    m_two,
    columns,
    scaled,
    grads,
    keep,
    z_out,
    z_in,
    norms,
    parts,
    part_sum,
    subs,
    merged,
    anchor_rows,
    outer_rows,
    gain_parts,
    gain_subs,
    local_sem,
    x_send,
    x_recv,
    c_send,
    c_recv,
    z_send,
    z_recv,
    q_send,
    q_recv,
    p_send,
    p_recv,
    l_send,
    l_recv,
):
    replicas = NP * NL
    rep = lax.axis_index("rep")
    my_part = rep % NP
    my_plane = rep // NP
    me = lax.axis_index("fsdp")
    my_z = me // NX
    my_x = me % NX

    def at(z, x):
        return {"fsdp": z * NX + x}

    def in_plane(k):
        return {"rep": my_plane * NP + (my_part + k) % NP}

    def over_planes(k):
        return {"rep": (my_plane + k) % NL * NP + my_part}

    def part_of(part):
        return pl.ds(pl.multiple_of(part * PART, PART), PART)

    sub_rows = pl.ds(pl.multiple_of(my_part * PART + my_plane * SUB, SUB), SUB)

    loads = []
    for place, (source, target) in enumerate(
        (
            (inputs.at[0], xin.at[0]),
            (cotangent, cin),
            (inputs.at[1], xin.at[1]),
            (weight, win),
            (adam_first, m_one),
            (adam_second, m_two),
            (anchor_weight.at[sub_rows], anchor_rows),
            (outer_weight.at[sub_rows], outer_rows),
        )
    ):
        copy = pltpu.make_async_copy(source, target, local_sem.at[place])
        copy.start()
        loads.append(copy)

    def column(j, i):
        owner = flip(my_z, j) * NX + flip(my_x, i)
        return pl.ds(pl.multiple_of(owner * ROWS, ROWS), ROWS)

    own_copies = {}
    place = len(loads)
    for s in range(INNER):
        for j in ORDER:
            copy = pltpu.make_async_copy(
                inputs.at[s, :, column(j, 0)],
                columns.at[s, j, pl.ds(0, TOK)],
                local_sem.at[place],
            )
            copy.start()
            own_copies[s, j] = copy
            place += 1

    barrier = pltpu.get_barrier_semaphore()
    for k in range(1, NF):
        pl.semaphore_signal(
            barrier, inc=1, device_id={"fsdp": (me + k) % NF}, device_id_type=MESH
        )
    for k in range(1, NP):
        pl.semaphore_signal(barrier, inc=1, device_id=in_plane(k), device_id_type=MESH)
    for k in range(1, NL):
        pl.semaphore_signal(barrier, inc=1, device_id=over_planes(k), device_id_type=MESH)
    pl.semaphore_wait(barrier, NF + NP + NL - 3)

    sends = []

    def send(source, target, send_sem, recv_sem, device):
        copy = pltpu.make_async_remote_copy(
            src_ref=source,
            dst_ref=target,
            send_sem=send_sem,
            recv_sem=recv_sem,
            device_id=device,
            device_id_type=MESH,
        )
        copy.start()
        sends.append(copy)
        return copy

    x_copies = {}
    c_copies = {}
    z_copies = {}
    q_copies = {}

    def send_columns(s, j):
        x_copies[s, j] = [
            send(
                inputs.at[s, :, column(j, i)],
                columns.at[s, j, pl.ds(i * TOK, TOK)],
                x_send.at[s, j, i - 1],
                x_recv.at[s, j, i - 1],
                at(my_z, flip(my_x, i)),
            )
            for i in (1, 3, 2)
        ]

    def send_scaled(s):
        values = xin[s].astype(jnp.float32)
        mean = jnp.mean(values * values, axis=-1, keepdims=True)
        scale = lax.rsqrt(mean + EPS_NORM)
        scaled[s, pl.ds(0, TOK), :] = (cin[s].astype(jnp.float32) * scale).astype(
            jnp.bfloat16
        )
        c_copies[s] = [
            send(
                scaled.at[s, pl.ds(0, TOK)],
                scaled.at[s, pl.ds(i * TOK, TOK)],
                c_send.at[s, i - 1],
                c_recv.at[s, i - 1],
                at(my_z, flip(my_x, i)),
            )
            for i in (1, 3, 2)
        ]

    def send_rows(s, slot, j):
        z_copies[s, slot] = send(
            z_out.at[s, slot],
            z_in.at[s, slot],
            z_send.at[s, slot],
            z_recv.at[s, slot],
            at(flip(my_z, j), my_x),
        )


    def exchange(stage, sems, count, source, target, device):
        return [
            send(
                source(k),
                target(k),
                sems[0].at[stage, k - 1],
                sems[1].at[stage, k - 1],
                device(k),
            )
            for k in range(1, count)
        ]

    planes = (p_send, p_recv), NP
    levels = (l_send, l_recv), NL

    def rep_start():
        return exchange(
            0,
            *planes,
            lambda k: weight.at[part_of((my_part + k) % NP)],
            lambda k: parts.at[k],
            in_plane,
        ) + exchange(1, *planes, lambda k: gains, lambda k: gain_parts.at[k], in_plane)

    def rep_second(copies):
        for copy in copies:
            copy.wait_recv()
        loads[3].wait()
        total = win[part_of(my_part), :]
        for k in range(1, NP):
            total = total + parts[k]
        part_sum[...] = total
        gain_total = gains[...]
        for k in range(1, NP):
            gain_total = gain_total + gain_parts[k]
        gain_subs[0] = gain_total
        return exchange(
            0,
            *levels,
            lambda k: part_sum.at[
                pl.ds(pl.multiple_of((my_plane + k) % NL * SUB, SUB), SUB)
            ],
            lambda k: subs.at[k],
            over_planes,
        ) + exchange(
            1, *levels, lambda k: gain_subs.at[0], lambda k: gain_subs.at[k], over_planes
        )

    def rep_third(copies):
        for copy in copies:
            copy.wait_recv()
        total = part_sum[pl.ds(pl.multiple_of(my_plane * SUB, SUB), SUB), :]
        for k in range(1, NL):
            total = total + subs[k]
        loads[6].wait()
        loads[7].wait()
        anchor = anchor_rows[...]
        merged[sub_rows, :] = outer_step(
            anchor, outer_rows[...], anchor - total / replicas
        )
        return exchange(
            2,
            *levels,
            lambda k: merged.at[sub_rows],
            lambda k: merged.at[sub_rows],
            over_planes,
        )

    def rep_fourth(copies):
        for copy in copies:
            copy.wait_recv()
        return exchange(
            2,
            *planes,
            lambda k: merged.at[part_of(my_part)],
            lambda k: merged.at[part_of(my_part)],
            in_plane,
        )

    chunks = [(s, j) for s in range(INNER) for j in ORDER]
    send_columns(*chunks[0])
    rep_copies = rep_start()
    loads[0].wait()
    loads[1].wait()
    send_scaled(0)
    send_columns(*chunks[1])
    loads[2].wait()

    low = pl.ds(0, HALF)
    high = pl.ds(HALF, HALF)

    def product(number):
        s, j = chunks[number]
        own_copies[s, j].wait()
        for copy in x_copies[s, j]:
            copy.wait_recv()
        if j == ORDER[0]:
            for copy in c_copies[s]:
                copy.wait_recv()
        if number + 2 < len(chunks):
            send_columns(*chunks[number + 2])
            if number == 1:
                send_scaled(1)
        block = lax.dot_general(
            columns[s, j],
            scaled[s],
            (((0,), (0,)), ((), ())),
            preferred_element_type=jnp.float32,
        )
        if j == 2:
            z_out[s, 0] = block[:HALF].astype(jnp.bfloat16)
            send_rows(s, 0, 1)
            z_out[s, 1] = block[HALF:].astype(jnp.bfloat16)
            send_rows(s, 1, 3)
        elif j == 1:
            z_out[s, 2] = block[:HALF].astype(jnp.bfloat16)
            send_rows(s, 2, 1)
            keep[s, 1] = block[HALF:]
        elif j == 3:
            z_out[s, 3] = block[HALF:].astype(jnp.bfloat16)
            send_rows(s, 3, 3)
            keep[s, 0] = block[:HALF]
        else:
            grads[s] = block

    def forward(s):
        z_copies[s, 0].wait_recv()
        z_out[s, 4] = (keep[s, 0] + z_in[s, 0].astype(jnp.float32)).astype(jnp.bfloat16)
        send_rows(s, 4, 3)
        z_copies[s, 1].wait_recv()
        z_out[s, 5] = (keep[s, 1] + z_in[s, 1].astype(jnp.float32)).astype(jnp.bfloat16)
        send_rows(s, 5, 1)

    def reduce_rows(s):
        for slot in (2, 3, 4, 5):
            z_copies[s, slot].wait_recv()
        grads[s, low] = grads[s, low] + (
            z_in[s, 2].astype(jnp.float32) + z_in[s, 4].astype(jnp.float32)
        )
        grads[s, high] = grads[s, high] + (
            z_in[s, 3].astype(jnp.float32) + z_in[s, 5].astype(jnp.float32)
        )

    def update(s, current, gain, moments, gain_moments):
        product_sum = grads[s]
        low_weight = current.astype(jnp.bfloat16).astype(jnp.float32)
        grad_gain = jnp.sum(product_sum * low_weight, axis=1, keepdims=True)
        grad_weight = product_sum * gain
        squares = grad_weight * grad_weight
        folded = squares[:, 0:128] + squares[:, 128:256] + squares[:, 256:384] + squares[:, 384:512]
        lane = lax.broadcasted_iota(jnp.int32, (ROWS, 128), 1)
        folded = folded + jnp.where(lane == 0, grad_gain * grad_gain, 0.0)
        norms[s, 0] = jnp.sum(folded.reshape(ROWS // 8, 8, 128), axis=0)
        q_copies[s] = [
            send(
                norms.at[s, 0],
                norms.at[s, k],
                q_send.at[s, k - 1],
                q_recv.at[s, k - 1],
                {"fsdp": (me + k) % NF},
            )
            for k in range(1, NF)
        ]
        for copy in q_copies[s]:
            copy.wait_recv()
        total = jnp.sum(jnp.sum(norms[s], axis=0), keepdims=True)
        factor = jnp.minimum(1.0, 1.0 / (jnp.sqrt(total) + 1e-06))
        current, one, two = adam_update(
            current, factor * grad_weight, moments[0], moments[1], DECAY
        )
        gain, gain_one, gain_two = adam_update(
            gain, factor * grad_gain, gain_moments[0], gain_moments[1], 0.0
        )
        return current, gain, (one, two), (gain_one, gain_two)

    product(0)
    product(1)
    rep_copies = rep_second(rep_copies)
    product(2)
    product(3)
    forward(0)
    rep_copies = rep_third(rep_copies)
    product(4)
    product(5)
    rep_copies = rep_fourth(rep_copies)
    product(6)
    product(7)
    for copy in loads[4:6]:
        copy.wait()
    turned = jnp.transpose(gains[...])
    reduce_rows(0)
    current, gain, moments, gain_moments = update(
        0,
        win[...],
        turned[:, 0:1],
        (m_one[...].astype(jnp.float32), m_two[...].astype(jnp.float32)),
        (turned[:, 1:2], turned[:, 2:3]),
    )
    forward(1)
    reduce_rows(1)
    current, gain, _, _ = update(1, current, gain, moments, gain_moments)
    for copy in rep_copies:
        copy.wait_recv()
    out_weight[...] = MIXING * current + (1.0 - MIXING) * merged[...]
    gain_total = gain_subs[0] + gain_subs[1] + gain_subs[2] + gain_subs[3]
    anchor_gain = gains[3:4, :]
    new_gain = outer_step(
        anchor_gain, gains[4:5, :], anchor_gain - gain_total[0:1, :] / replicas
    )
    gain_row = jnp.transpose(jnp.broadcast_to(gain, (ROWS, 8)))
    out_gain[...] = MIXING * gain_row[0:1, :] + (1.0 - MIXING) * new_gain
    for copy in sends:
        copy.wait_send()


def window(
    inputs, cotangent, weight, adam_first, adam_second, anchor_weight, outer_weight, gains
):
    anywhere = pl.BlockSpec(memory_space=pl.ANY)
    vmem = pl.BlockSpec(memory_space=pltpu.VMEM)
    dma = pltpu.SemaphoreType.DMA
    f32, bf16 = jnp.float32, jnp.bfloat16
    return pl.pallas_call(
        kernel,
        out_shape=(
            jax.ShapeDtypeStruct((ROWS, KW), f32),
            jax.ShapeDtypeStruct((1, ROWS), f32),
        ),
        in_specs=[anywhere] * 7 + [vmem],
        out_specs=(vmem, vmem),
        scratch_shapes=[
            pltpu.VMEM((INNER, TOK, D), bf16),
            pltpu.VMEM((INNER, TOK, KW), bf16),
            pltpu.VMEM((ROWS, KW), f32),
            pltpu.VMEM((ROWS, KW), bf16),
            pltpu.VMEM((ROWS, KW), bf16),
            pltpu.VMEM((INNER, NZ, NX * TOK, ROWS), bf16),
            pltpu.VMEM((INNER, NX * TOK, KW), bf16),
            pltpu.VMEM((INNER, ROWS, KW), f32),
            pltpu.VMEM((INNER, 2, HALF, KW), f32),
            pltpu.VMEM((INNER, 6, HALF, KW), bf16),
            pltpu.VMEM((INNER, 6, HALF, KW), bf16),
            pltpu.VMEM((INNER, NF, 8, 128), f32),
            pltpu.VMEM((NP, PART, KW), f32),
            pltpu.VMEM((PART, KW), f32),
            pltpu.VMEM((NL, SUB, KW), f32),
            pltpu.VMEM((ROWS, KW), f32),
            pltpu.VMEM((SUB, KW), f32),
            pltpu.VMEM((SUB, KW), f32),
            pltpu.VMEM((NP, 8, ROWS), f32),
            pltpu.VMEM((NL, 8, ROWS), f32),
            dma((8 + INNER * NZ,)),
            dma((INNER, NZ, NX - 1)),
            dma((INNER, NZ, NX - 1)),
            dma((INNER, NX - 1)),
            dma((INNER, NX - 1)),
            dma((INNER, 6)),
            dma((INNER, 6)),
            dma((INNER, NF - 1)),
            dma((INNER, NF - 1)),
            dma((3, NP - 1)),
            dma((3, NP - 1)),
            dma((3, NL - 1)),
            dma((3, NL - 1)),
        ],
        compiler_params=pltpu.CompilerParams(
            collective_id=0, has_side_effects=True, vmem_limit_bytes=40 * 1024 * 1024
        ),
        cost_estimate=pl.CostEstimate(
            flops=4 * INNER * NX * TOK * NZ * ROWS * KW,
            bytes_accessed=8 * 1024 * 1024,
            transcendentals=0,
        ),
        name="inner_window",
    )(
        inputs, cotangent, weight, adam_first, adam_second, anchor_weight, outer_weight, gains
    )


def on_device(
    inputs,
    cotangent,
    weight,
    norm_gain,
    adam_first,
    adam_second,
    gain_first,
    gain_second,
    anchor_weight,
    anchor_gain,
    outer_weight,
    outer_gain,
):
    gains = jnp.concatenate(
        (
            norm_gain,
            gain_first,
            gain_second,
            anchor_gain[None],
            outer_gain[None],
            jnp.zeros((3, ROWS), jnp.float32),
        ),
        axis=0,
    )
    merged_weight, merged_gain = window(
        inputs,
        cotangent,
        weight[0],
        adam_first[0],
        adam_second[0],
        anchor_weight,
        outer_weight,
        gains,
    )
    return (merged_weight[None], merged_gain)


def solution(mesh):
    return jax.shard_map(
        on_device,
        mesh=mesh,
        in_specs=(
            P(None, ("rep", "fsdp"), None),
            P(None, ("rep", "fsdp"), None),
            P("rep", "fsdp", None),
            P("rep", "fsdp"),
            P("rep", "fsdp", None),
            P("rep", "fsdp", None),
            P("rep", "fsdp"),
            P("rep", "fsdp"),
            P("fsdp", None),
            P("fsdp"),
            P("fsdp", None),
            P("fsdp"),
        ),
        out_specs=(P("rep", "fsdp", None), P("rep", "fsdp")),
        check_vma=False,
    )
```

```python
import jax
import jax.numpy as jnp
from jax import lax
from jax.experimental import pallas as pl
from jax.experimental.pallas import tpu as pltpu
from jax.sharding import PartitionSpec as P

BETA_ONE = 0.9
BETA_TWO = 0.999
EPS_ADAM = 1e-08
RATE = 0.3
DECAY = 0.1
EPS_NORM = 1e-05
OUTER_RATE = 0.7
MOMENTUM = 0.9
MIXING = 0.5

INNER = 2
NX = 4
NZ = 4
NF = NX * NZ
TOK = 128
ROWS = 256
HALF = ROWS // 2
D = ROWS * NF
KW = 512
NP = 8
NL = 4
PART = ROWS // NP
SUB = PART // NL
ORDER = (2, 1, 3, 0)

MESH = pl.DeviceIdType.MESH


def flip(value, bits):
    if bits == 0:
        return value
    if bits == 1:
        return value + 1 - 2 * (value % 2)
    if bits == 2:
        return (value + 2) % 4
    return 3 - value


def adam_update(current, gradient, moment_one, moment_two, decay_rate):
    moment_one = BETA_ONE * moment_one + (1.0 - BETA_ONE) * gradient
    moment_two = BETA_TWO * moment_two + (1.0 - BETA_TWO) * gradient * gradient
    current = current - RATE * (
        moment_one / (jnp.sqrt(moment_two) + EPS_ADAM) + decay_rate * current
    )
    return (current, moment_one, moment_two)


def outer_step(anchor, momentum, mean_delta):
    velocity = MOMENTUM * momentum + mean_delta
    return anchor - OUTER_RATE * (mean_delta + MOMENTUM * velocity)


def kernel(
    inputs,
    cotangent,
    weight,
    adam_first,
    adam_second,
    anchor_weight,
    outer_weight,
    norm_gain,
    gain_first,
    gain_second,
    anchor_gain,
    outer_gain,
    out_weight,
    out_gain,
    xin,
    cin,
    win,
    m_one,
    m_two,
    columns,
    scaled,
    grads,
    keep,
    z_out,
    z_in,
    norms,
    parts,
    part_sum,
    subs,
    merged,
    anchor_rows,
    outer_rows,
    gain_in,
    gains,
    gain_parts,
    gain_subs,
    local_sem,
    x_send,
    x_recv,
    c_send,
    c_recv,
    z_send,
    z_recv,
    q_send,
    q_recv,
    p_send,
    p_recv,
    l_send,
    l_recv,
):
    replicas = NP * NL
    rep = lax.axis_index("rep")
    my_part = rep % NP
    my_plane = rep // NP
    me = lax.axis_index("fsdp")
    my_z = me // NX
    my_x = me % NX

    def at(z, x):
        return {"fsdp": z * NX + x}

    def in_plane(k):
        return {"rep": my_plane * NP + (my_part + k) % NP}

    def over_planes(k):
        return {"rep": (my_plane + k) % NL * NP + my_part}

    def part_of(part):
        return pl.ds(pl.multiple_of(part * PART, PART), PART)

    sub_rows = pl.ds(pl.multiple_of(my_part * PART + my_plane * SUB, SUB), SUB)

    loads = []
    for place, (source, target) in enumerate(
        (
            (inputs.at[0], xin.at[0]),
            (cotangent, cin),
            (inputs.at[1], xin.at[1]),
            (weight, win),
            (adam_first, m_one),
            (adam_second, m_two),
            (anchor_weight.at[sub_rows], anchor_rows),
            (outer_weight.at[sub_rows], outer_rows),
            (norm_gain, gain_in.at[0]),
            (gain_first, gain_in.at[1]),
            (gain_second, gain_in.at[2]),
            (anchor_gain, gain_in.at[3]),
            (outer_gain, gain_in.at[4]),
        )
    ):
        copy = pltpu.make_async_copy(source, target, local_sem.at[place])
        copy.start()
        loads.append(copy)

    def column(j, i):
        owner = flip(my_z, j) * NX + flip(my_x, i)
        return pl.ds(pl.multiple_of(owner * ROWS, ROWS), ROWS)

    own_copies = {}
    place = len(loads)
    for s in range(INNER):
        for j in ORDER:
            copy = pltpu.make_async_copy(
                inputs.at[s, :, column(j, 0)],
                columns.at[s, j, pl.ds(0, TOK)],
                local_sem.at[place],
            )
            copy.start()
            own_copies[s, j] = copy
            place += 1

    barrier = pltpu.get_barrier_semaphore()
    for k in range(1, NF):
        pl.semaphore_signal(
            barrier, inc=1, device_id={"fsdp": (me + k) % NF}, device_id_type=MESH
        )
    for k in range(1, NP):
        pl.semaphore_signal(barrier, inc=1, device_id=in_plane(k), device_id_type=MESH)
    for k in range(1, NL):
        pl.semaphore_signal(barrier, inc=1, device_id=over_planes(k), device_id_type=MESH)
    pl.semaphore_wait(barrier, NF + NP + NL - 3)

    sends = []

    def send(source, target, send_sem, recv_sem, device):
        copy = pltpu.make_async_remote_copy(
            src_ref=source,
            dst_ref=target,
            send_sem=send_sem,
            recv_sem=recv_sem,
            device_id=device,
            device_id_type=MESH,
        )
        copy.start()
        sends.append(copy)
        return copy

    x_copies = {}
    c_copies = {}
    z_copies = {}
    q_copies = {}

    def send_columns(s, j):
        x_copies[s, j] = [
            send(
                inputs.at[s, :, column(j, i)],
                columns.at[s, j, pl.ds(i * TOK, TOK)],
                x_send.at[s, j, i - 1],
                x_recv.at[s, j, i - 1],
                at(my_z, flip(my_x, i)),
            )
            for i in (1, 3, 2)
        ]

    def send_scaled(s):
        values = xin[s].astype(jnp.float32)
        mean = jnp.mean(values * values, axis=-1, keepdims=True)
        scale = lax.rsqrt(mean + EPS_NORM)
        scaled[s, pl.ds(0, TOK), :] = (cin[s].astype(jnp.float32) * scale).astype(
            jnp.bfloat16
        )
        c_copies[s] = [
            send(
                scaled.at[s, pl.ds(0, TOK)],
                scaled.at[s, pl.ds(i * TOK, TOK)],
                c_send.at[s, i - 1],
                c_recv.at[s, i - 1],
                at(my_z, flip(my_x, i)),
            )
            for i in (1, 3, 2)
        ]

    def send_rows(s, slot, j):
        z_copies[s, slot] = send(
            z_out.at[s, slot],
            z_in.at[s, slot],
            z_send.at[s, slot],
            z_recv.at[s, slot],
            at(flip(my_z, j), my_x),
        )


    def exchange(stage, sems, count, source, target, device):
        return [
            send(
                source(k),
                target(k),
                sems[0].at[stage, k - 1],
                sems[1].at[stage, k - 1],
                device(k),
            )
            for k in range(1, count)
        ]

    planes = (p_send, p_recv), NP
    levels = (l_send, l_recv), NL

    def rep_start():
        return exchange(
            0,
            *planes,
            lambda k: weight.at[part_of((my_part + k) % NP)],
            lambda k: parts.at[k],
            in_plane,
        ) + exchange(1, *planes, lambda k: gains, lambda k: gain_parts.at[k], in_plane)

    def rep_second(copies):
        for copy in copies:
            copy.wait_recv()
        loads[3].wait()
        total = win[part_of(my_part), :]
        for k in range(1, NP):
            total = total + parts[k]
        part_sum[...] = total
        gain_total = gains[...]
        for k in range(1, NP):
            gain_total = gain_total + gain_parts[k]
        gain_subs[0] = gain_total
        return exchange(
            0,
            *levels,
            lambda k: part_sum.at[
                pl.ds(pl.multiple_of((my_plane + k) % NL * SUB, SUB), SUB)
            ],
            lambda k: subs.at[k],
            over_planes,
        ) + exchange(
            1, *levels, lambda k: gain_subs.at[0], lambda k: gain_subs.at[k], over_planes
        )

    def rep_third(copies):
        for copy in copies:
            copy.wait_recv()
        total = part_sum[pl.ds(pl.multiple_of(my_plane * SUB, SUB), SUB), :]
        for k in range(1, NL):
            total = total + subs[k]
        loads[6].wait()
        loads[7].wait()
        anchor = anchor_rows[...]
        merged[sub_rows, :] = outer_step(
            anchor, outer_rows[...], anchor - total / replicas
        )
        return exchange(
            2,
            *levels,
            lambda k: merged.at[sub_rows],
            lambda k: merged.at[sub_rows],
            over_planes,
        )

    def rep_fourth(copies):
        for copy in copies:
            copy.wait_recv()
        return exchange(
            2,
            *planes,
            lambda k: merged.at[part_of(my_part)],
            lambda k: merged.at[part_of(my_part)],
            in_plane,
        )

    chunks = [(s, j) for s in range(INNER) for j in ORDER]
    send_columns(*chunks[0])
    for copy in loads[8:]:
        copy.wait()
    gains[...] = jnp.concatenate(
        [gain_in[k] for k in range(5)] + [jnp.zeros((3, ROWS), jnp.float32)], axis=0
    )
    rep_copies = rep_start()
    loads[0].wait()
    loads[1].wait()
    send_scaled(0)
    send_columns(*chunks[1])
    loads[2].wait()

    low = pl.ds(0, HALF)
    high = pl.ds(HALF, HALF)

    def product(number):
        s, j = chunks[number]
        own_copies[s, j].wait()
        for copy in x_copies[s, j]:
            copy.wait_recv()
        if j == ORDER[0]:
            for copy in c_copies[s]:
                copy.wait_recv()
        if number + 2 < len(chunks):
            send_columns(*chunks[number + 2])
            if number == 1:
                send_scaled(1)
        block = lax.dot_general(
            columns[s, j],
            scaled[s],
            (((0,), (0,)), ((), ())),
            preferred_element_type=jnp.float32,
        )
        if j == 2:
            z_out[s, 0] = block[:HALF].astype(jnp.bfloat16)
            send_rows(s, 0, 1)
            z_out[s, 1] = block[HALF:].astype(jnp.bfloat16)
            send_rows(s, 1, 3)
        elif j == 1:
            z_out[s, 2] = block[:HALF].astype(jnp.bfloat16)
            send_rows(s, 2, 1)
            keep[s, 1] = block[HALF:]
        elif j == 3:
            z_out[s, 3] = block[HALF:].astype(jnp.bfloat16)
            send_rows(s, 3, 3)
            keep[s, 0] = block[:HALF]
        else:
            grads[s] = block

    def forward(s):
        z_copies[s, 0].wait_recv()
        z_out[s, 4] = (keep[s, 0] + z_in[s, 0].astype(jnp.float32)).astype(jnp.bfloat16)
        send_rows(s, 4, 3)
        z_copies[s, 1].wait_recv()
        z_out[s, 5] = (keep[s, 1] + z_in[s, 1].astype(jnp.float32)).astype(jnp.bfloat16)
        send_rows(s, 5, 1)

    def reduce_rows(s):
        for slot in (2, 3, 4, 5):
            z_copies[s, slot].wait_recv()
        grads[s, low] = grads[s, low] + (
            z_in[s, 2].astype(jnp.float32) + z_in[s, 4].astype(jnp.float32)
        )
        grads[s, high] = grads[s, high] + (
            z_in[s, 3].astype(jnp.float32) + z_in[s, 5].astype(jnp.float32)
        )

    def update(s, current, gain, moments, gain_moments):
        product_sum = grads[s]
        low_weight = current.astype(jnp.bfloat16).astype(jnp.float32)
        grad_gain = jnp.sum(product_sum * low_weight, axis=1, keepdims=True)
        grad_weight = product_sum * gain
        squares = grad_weight * grad_weight
        folded = squares[:, 0:128] + squares[:, 128:256] + squares[:, 256:384] + squares[:, 384:512]
        lane = lax.broadcasted_iota(jnp.int32, (ROWS, 128), 1)
        folded = folded + jnp.where(lane == 0, grad_gain * grad_gain, 0.0)
        norms[s, 0] = jnp.sum(folded.reshape(ROWS // 8, 8, 128), axis=0)
        q_copies[s] = [
            send(
                norms.at[s, 0],
                norms.at[s, k],
                q_send.at[s, k - 1],
                q_recv.at[s, k - 1],
                {"fsdp": (me + k) % NF},
            )
            for k in range(1, NF)
        ]
        for copy in q_copies[s]:
            copy.wait_recv()
        total = jnp.sum(jnp.sum(norms[s], axis=0), keepdims=True)
        factor = jnp.minimum(1.0, 1.0 / (jnp.sqrt(total) + 1e-06))
        current, one, two = adam_update(
            current, factor * grad_weight, moments[0], moments[1], DECAY
        )
        gain, gain_one, gain_two = adam_update(
            gain, factor * grad_gain, gain_moments[0], gain_moments[1], 0.0
        )
        return current, gain, (one, two), (gain_one, gain_two)

    product(0)
    product(1)
    rep_copies = rep_second(rep_copies)
    product(2)
    product(3)
    forward(0)
    rep_copies = rep_third(rep_copies)
    product(4)
    product(5)
    rep_copies = rep_fourth(rep_copies)
    product(6)
    product(7)
    for copy in loads[4:6]:
        copy.wait()
    turned = jnp.transpose(gains[...])
    reduce_rows(0)
    current, gain, moments, gain_moments = update(
        0,
        win[...],
        turned[:, 0:1],
        (m_one[...].astype(jnp.float32), m_two[...].astype(jnp.float32)),
        (turned[:, 1:2], turned[:, 2:3]),
    )
    forward(1)
    reduce_rows(1)
    current, gain, _, _ = update(1, current, gain, moments, gain_moments)
    for copy in rep_copies:
        copy.wait_recv()
    out_weight[...] = MIXING * current + (1.0 - MIXING) * merged[...]
    gain_total = gain_subs[0]
    for k in range(1, NL):
        gain_total = gain_total + gain_subs[k]
    anchor_row = gains[3:4, :]
    new_gain = outer_step(
        anchor_row, gains[4:5, :], anchor_row - gain_total[0:1, :] / replicas
    )
    gain_row = jnp.transpose(jnp.broadcast_to(gain, (ROWS, 8)))
    out_gain[...] = MIXING * gain_row[0:1, :] + (1.0 - MIXING) * new_gain
    for copy in sends:
        copy.wait_send()


def window(*operands):
    anywhere = pl.BlockSpec(memory_space=pl.ANY)
    vmem = pl.BlockSpec(memory_space=pltpu.VMEM)
    dma = pltpu.SemaphoreType.DMA
    f32, bf16 = jnp.float32, jnp.bfloat16
    return pl.pallas_call(
        kernel,
        out_shape=(
            jax.ShapeDtypeStruct((ROWS, KW), f32),
            jax.ShapeDtypeStruct((1, ROWS), f32),
        ),
        in_specs=[anywhere] * len(operands),
        out_specs=(vmem, vmem),
        scratch_shapes=[
            pltpu.VMEM((INNER, TOK, D), bf16),
            pltpu.VMEM((INNER, TOK, KW), bf16),
            pltpu.VMEM((ROWS, KW), f32),
            pltpu.VMEM((ROWS, KW), bf16),
            pltpu.VMEM((ROWS, KW), bf16),
            pltpu.VMEM((INNER, NZ, NX * TOK, ROWS), bf16),
            pltpu.VMEM((INNER, NX * TOK, KW), bf16),
            pltpu.VMEM((INNER, ROWS, KW), f32),
            pltpu.VMEM((INNER, 2, HALF, KW), f32),
            pltpu.VMEM((INNER, 6, HALF, KW), bf16),
            pltpu.VMEM((INNER, 6, HALF, KW), bf16),
            pltpu.VMEM((INNER, NF, 8, 128), f32),
            pltpu.VMEM((NP, PART, KW), f32),
            pltpu.VMEM((PART, KW), f32),
            pltpu.VMEM((NL, SUB, KW), f32),
            pltpu.VMEM((ROWS, KW), f32),
            pltpu.VMEM((SUB, KW), f32),
            pltpu.VMEM((SUB, KW), f32),
            pltpu.VMEM((5, 1, ROWS), f32),
            pltpu.VMEM((8, ROWS), f32),
            pltpu.VMEM((NP, 8, ROWS), f32),
            pltpu.VMEM((NL, 8, ROWS), f32),
            dma((13 + INNER * NZ,)),
            dma((INNER, NZ, NX - 1)),
            dma((INNER, NZ, NX - 1)),
            dma((INNER, NX - 1)),
            dma((INNER, NX - 1)),
            dma((INNER, 6)),
            dma((INNER, 6)),
            dma((INNER, NF - 1)),
            dma((INNER, NF - 1)),
            dma((3, NP - 1)),
            dma((3, NP - 1)),
            dma((3, NL - 1)),
            dma((3, NL - 1)),
        ],
        compiler_params=pltpu.CompilerParams(
            collective_id=0, has_side_effects=True, vmem_limit_bytes=60 * 1024 * 1024
        ),
        cost_estimate=pl.CostEstimate(
            flops=4 * INNER * NX * TOK * NZ * ROWS * KW,
            bytes_accessed=8 * 1024 * 1024,
            transcendentals=0,
        ),
        name="inner_window",
    )(*operands)


def on_device(
    inputs,
    cotangent,
    weight,
    norm_gain,
    adam_first,
    adam_second,
    gain_first,
    gain_second,
    anchor_weight,
    anchor_gain,
    outer_weight,
    outer_gain,
):
    merged_weight, merged_gain = window(
        inputs,
        cotangent,
        weight[0],
        adam_first[0],
        adam_second[0],
        anchor_weight,
        outer_weight,
        norm_gain,
        gain_first,
        gain_second,
        anchor_gain[None],
        outer_gain[None],
    )
    return (merged_weight[None], merged_gain)


def solution(mesh):
    return jax.shard_map(
        on_device,
        mesh=mesh,
        in_specs=(
            P(None, ("rep", "fsdp"), None),
            P(None, ("rep", "fsdp"), None),
            P("rep", "fsdp", None),
            P("rep", "fsdp"),
            P("rep", "fsdp", None),
            P("rep", "fsdp", None),
            P("rep", "fsdp"),
            P("rep", "fsdp"),
            P("fsdp", None),
            P("fsdp"),
            P("fsdp", None),
            P("fsdp"),
        ),
        out_specs=(P("rep", "fsdp", None), P("rep", "fsdp")),
        check_vma=False,
    )
```

```python
import jax
import jax.numpy as jnp
from jax import lax
from jax.experimental import pallas as pl
from jax.experimental.pallas import tpu as pltpu
from jax.sharding import PartitionSpec as P

BETA_ONE = 0.9
BETA_TWO = 0.999
EPS_ADAM = 1e-08
RATE = 0.3
DECAY = 0.1
EPS_NORM = 1e-05
OUTER_RATE = 0.7
MOMENTUM = 0.9
MIXING = 0.5

INNER = 2
NX = 4
NZ = 4
NF = NX * NZ
TOK = 128
ROWS = 256
HALF = ROWS // 2
D = ROWS * NF
KW = 512
NP = 8
NL = 4
PART = ROWS // NP
SUB = PART // NL
ORDER = (2, 1, 3, 0)

MESH = pl.DeviceIdType.MESH


def flip(value, bits):
    if bits == 0:
        return value
    if bits == 1:
        return value + 1 - 2 * (value % 2)
    if bits == 2:
        return (value + 2) % 4
    return 3 - value


def adam_update(current, gradient, moment_one, moment_two, decay_rate):
    moment_one = BETA_ONE * moment_one + (1.0 - BETA_ONE) * gradient
    moment_two = BETA_TWO * moment_two + (1.0 - BETA_TWO) * gradient * gradient
    current = current - RATE * (
        moment_one / (jnp.sqrt(moment_two) + EPS_ADAM) + decay_rate * current
    )
    return (current, moment_one, moment_two)


def outer_step(anchor, momentum, mean_delta):
    velocity = MOMENTUM * momentum + mean_delta
    return anchor - OUTER_RATE * (mean_delta + MOMENTUM * velocity)


def kernel(
    inputs,
    cotangent,
    weight,
    adam_first,
    adam_second,
    anchor_weight,
    outer_weight,
    norm_gain,
    gain_first,
    gain_second,
    anchor_gain,
    outer_gain,
    out_weight,
    out_gain,
    xin,
    cin,
    win,
    m_one,
    m_two,
    columns,
    scaled,
    grads,
    keep,
    z_out,
    z_in,
    norms,
    parts,
    part_sum,
    subs,
    merged,
    anchor_rows,
    outer_rows,
    gain_in,
    gains,
    gain_parts,
    gain_subs,
    local_sem,
    x_send,
    x_recv,
    c_send,
    c_recv,
    z_send,
    z_recv,
    q_send,
    q_recv,
    p_send,
    p_recv,
    l_send,
    l_recv,
):
    replicas = NP * NL
    rep = lax.axis_index("rep")
    my_part = rep % NP
    my_plane = rep // NP
    me = lax.axis_index("fsdp")
    my_z = me // NX
    my_x = me % NX

    def at(z, x):
        return {"fsdp": z * NX + x}

    def in_plane(k):
        return {"rep": my_plane * NP + (my_part + k) % NP}

    def over_planes(k):
        return {"rep": (my_plane + k) % NL * NP + my_part}

    barrier = pltpu.get_barrier_semaphore()
    for k in range(1, NF):
        pl.semaphore_signal(
            barrier, inc=1, device_id={"fsdp": (me + k) % NF}, device_id_type=MESH
        )
    for k in range(1, NP):
        pl.semaphore_signal(barrier, inc=1, device_id=in_plane(k), device_id_type=MESH)
    for k in range(1, NL):
        pl.semaphore_signal(barrier, inc=1, device_id=over_planes(k), device_id_type=MESH)

    def part_of(part):
        return pl.ds(pl.multiple_of(part * PART, PART), PART)

    sub_rows = pl.ds(pl.multiple_of(my_part * PART + my_plane * SUB, SUB), SUB)

    loads = []
    for place, (source, target) in enumerate(
        (
            (inputs.at[0], xin.at[0]),
            (cotangent, cin),
            (inputs.at[1], xin.at[1]),
            (weight, win),
            (adam_first, m_one),
            (adam_second, m_two),
            (anchor_weight.at[sub_rows], anchor_rows),
            (outer_weight.at[sub_rows], outer_rows),
            (norm_gain, gain_in.at[0]),
            (gain_first, gain_in.at[1]),
            (gain_second, gain_in.at[2]),
            (anchor_gain, gain_in.at[3]),
            (outer_gain, gain_in.at[4]),
        )
    ):
        copy = pltpu.make_async_copy(source, target, local_sem.at[place])
        copy.start()
        loads.append(copy)

    def column(j, i):
        owner = flip(my_z, j) * NX + flip(my_x, i)
        return pl.ds(pl.multiple_of(owner * ROWS, ROWS), ROWS)

    own_copies = {}
    place = len(loads)
    for s in range(INNER):
        for j in ORDER:
            copy = pltpu.make_async_copy(
                inputs.at[s, :, column(j, 0)],
                columns.at[s, j, pl.ds(0, TOK)],
                local_sem.at[place],
            )
            copy.start()
            own_copies[s, j] = copy
            place += 1

    sends = []

    def send(source, target, send_sem, recv_sem, device):
        copy = pltpu.make_async_remote_copy(
            src_ref=source,
            dst_ref=target,
            send_sem=send_sem,
            recv_sem=recv_sem,
            device_id=device,
            device_id_type=MESH,
        )
        copy.start()
        sends.append(copy)
        return copy

    x_copies = {}
    c_copies = {}
    z_copies = {}
    q_copies = {}

    def send_columns(s, j):
        x_copies[s, j] = [
            send(
                inputs.at[s, :, column(j, i)],
                columns.at[s, j, pl.ds(i * TOK, TOK)],
                x_send.at[s, j, i - 1],
                x_recv.at[s, j, i - 1],
                at(my_z, flip(my_x, i)),
            )
            for i in (1, 3, 2)
        ]

    def scale(s):
        values = xin[s].astype(jnp.float32)
        mean = jnp.mean(values * values, axis=-1, keepdims=True)
        scale = lax.rsqrt(mean + EPS_NORM)
        scaled[s, pl.ds(0, TOK), :] = (cin[s].astype(jnp.float32) * scale).astype(
            jnp.bfloat16
        )

    def send_scaled(s, part, width):
        columns_of = pl.ds(part * width, width)
        c_copies[s, part] = [
            send(
                scaled.at[s, pl.ds(0, TOK), columns_of],
                scaled.at[s, pl.ds(i * TOK, TOK), columns_of],
                c_send.at[s, part, i - 1],
                c_recv.at[s, part, i - 1],
                at(my_z, flip(my_x, i)),
            )
            for i in (1, 3, 2)
        ]

    def send_rows(s, slot, j, part=0, width=KW):
        columns_of = pl.ds(part * width, width)
        sem = slot + 6 * part
        z_copies[s, sem] = send(
            z_out.at[s, slot, :, columns_of],
            z_in.at[s, slot, :, columns_of],
            z_send.at[s, sem],
            z_recv.at[s, sem],
            at(flip(my_z, j), my_x),
        )

    def sent(s, *slots):
        for slot in slots:
            copy = z_copies[s, slot]
            copy.wait_send()
            sends[:] = [other for other in sends if other is not copy]


    def exchange(stage, sems, count, source, target, device):
        return [
            send(
                source(k),
                target(k),
                sems[0].at[stage, k - 1],
                sems[1].at[stage, k - 1],
                device(k),
            )
            for k in range(1, count)
        ]

    planes = (p_send, p_recv), NP
    levels = (l_send, l_recv), NL

    def rep_start():
        return exchange(
            0,
            *planes,
            lambda k: weight.at[part_of((my_part + k) % NP)],
            lambda k: parts.at[k],
            in_plane,
        ) + exchange(
            1, *planes, lambda k: gain_in.at[0], lambda k: gain_parts.at[k], in_plane
        )

    def rep_second(copies):
        for copy in copies:
            copy.wait_recv()
        loads[3].wait()
        total = win[part_of(my_part), :]
        for k in range(1, NP):
            total = total + parts[k]
        part_sum[...] = total
        gain_total = gain_in[0]
        for k in range(1, NP):
            gain_total = gain_total + gain_parts[k]
        gain_subs[0] = gain_total
        return exchange(
            0,
            *levels,
            lambda k: part_sum.at[
                pl.ds(pl.multiple_of((my_plane + k) % NL * SUB, SUB), SUB)
            ],
            lambda k: subs.at[k],
            over_planes,
        ) + exchange(
            1, *levels, lambda k: gain_subs.at[0], lambda k: gain_subs.at[k], over_planes
        )

    def rep_third(copies):
        for copy in copies:
            copy.wait_recv()
        total = part_sum[pl.ds(pl.multiple_of(my_plane * SUB, SUB), SUB), :]
        for k in range(1, NL):
            total = total + subs[k]
        loads[6].wait()
        loads[7].wait()
        anchor = anchor_rows[...]
        merged[sub_rows, :] = outer_step(
            anchor, outer_rows[...], anchor - total / replicas
        )
        return exchange(
            2,
            *levels,
            lambda k: merged.at[sub_rows],
            lambda k: merged.at[sub_rows],
            over_planes,
        )

    def rep_fourth(copies):
        for copy in copies:
            copy.wait_recv()
        return exchange(
            2,
            *planes,
            lambda k: merged.at[part_of(my_part)],
            lambda k: merged.at[part_of(my_part)],
            in_plane,
        )

    low = pl.ds(0, HALF)
    high = pl.ds(HALF, HALF)

    def multiply(s, j, columns_of):
        return lax.dot_general(
            columns[s, j],
            scaled[s, :, columns_of],
            (((0,), (0,)), ((), ())),
            preferred_element_type=jnp.float32,
        )

    def arrived(s, j, part=None):
        if part in (None, 0):
            own_copies[s, j].wait()
            for copy in x_copies[s, j]:
                copy.wait_recv()
        if part is not None:
            for copy in c_copies[s, part]:
                copy.wait_recv()

    def first_product(s, parts_of):
        width = KW // parts_of
        for part in range(parts_of):
            arrived(s, 2, part)
            columns_of = pl.ds(part * width, width)
            block = multiply(s, 2, columns_of)
            z_out[s, 0, :, columns_of] = block[:HALF].astype(jnp.bfloat16)
            z_out[s, 1, :, columns_of] = block[HALF:].astype(jnp.bfloat16)
            if s == 0:
                send_rows(s, 0, 1, part, width)
                send_rows(s, 1, 3, part, width)

    def product(s, j):
        arrived(s, j)
        block = multiply(s, j, pl.ds(0, KW))
        if j == 1:
            z_out[s, 2] = block[:HALF].astype(jnp.bfloat16)
            keep[s, 1] = block[HALF:]
        elif j == 3:
            z_out[s, 3] = block[HALF:].astype(jnp.bfloat16)
            keep[s, 0] = block[:HALF]
        else:
            grads[s] = block

    def forward(s):
        for slot, target, j in ((0, 4, 3), (1, 5, 1)):
            z_copies[s, slot].wait_recv()
            z_copies[s, slot + 6].wait_recv()
            total = keep[s, slot] + z_in[s, slot].astype(jnp.float32)
            z_out[s, target] = total.astype(jnp.bfloat16)
            send_rows(s, target, j)

    def reduce_rows(s):
        for slot in (2, 3, 4, 5):
            z_copies[s, slot].wait_recv()
        grads[s, low] = grads[s, low] + (
            z_in[s, 2].astype(jnp.float32) + z_in[s, 4].astype(jnp.float32)
        )
        grads[s, high] = grads[s, high] + (
            z_in[s, 3].astype(jnp.float32) + z_in[s, 5].astype(jnp.float32)
        )

    def send_norm(s, current, gain):
        product_sum = grads[s]
        low_weight = current.astype(jnp.bfloat16).astype(jnp.float32)
        grad_gain = jnp.sum(product_sum * low_weight, axis=1, keepdims=True)
        grad_weight = product_sum * gain
        squares = grad_weight * grad_weight
        folded = squares[:, 0:128] + squares[:, 128:256] + squares[:, 256:384] + squares[:, 384:512]
        lane = lax.broadcasted_iota(jnp.int32, (ROWS, 128), 1)
        folded = folded + jnp.where(lane == 0, grad_gain * grad_gain, 0.0)
        norms[s, 0] = jnp.sum(folded, axis=0, keepdims=True)
        q_copies[s] = [
            send(
                norms.at[s, 0],
                norms.at[s, k],
                q_send.at[s, k - 1],
                q_recv.at[s, k - 1],
                {"fsdp": (me + k) % NF},
            )
            for k in range(1, NF)
        ]
        return grad_gain

    def update(s, current, gain, grad_gain, moments, gain_moments):
        for copy in q_copies[s]:
            copy.wait_recv()
        total = jnp.sum(jnp.sum(norms[s], axis=0), keepdims=True)
        factor = jnp.minimum(1.0, 1.0 / (jnp.sqrt(total) + 1e-06))
        current, one, two = adam_update(
            current, factor * (grads[s] * gain), moments[0], moments[1], DECAY
        )
        gain, gain_one, gain_two = adam_update(
            gain, factor * grad_gain, gain_moments[0], gain_moments[1], 0.0
        )
        return current, gain, (one, two), (gain_one, gain_two)

    pl.semaphore_wait(barrier, NF + NP + NL - 3)

    send_columns(0, 2)
    for copy in loads[:2]:
        copy.wait()
    scale(0)
    send_scaled(0, 0, KW // 2)
    send_scaled(0, 1, KW // 2)
    for copy in loads[8:]:
        copy.wait()
    gains[...] = jnp.concatenate(
        [gain_in[k] for k in range(5)] + [jnp.zeros((3, ROWS), jnp.float32)], axis=0
    )
    rep_copies = rep_start()
    send_columns(0, 1)
    first_product(0, 2)
    send_columns(0, 3)
    send_columns(0, 0)
    product(0, 1)
    send_rows(0, 2, 1)
    loads[2].wait()
    scale(1)
    send_scaled(1, 0, KW)
    send_columns(1, 2)
    product(0, 3)
    send_rows(0, 3, 3)
    product(0, 0)
    send_columns(1, 1)
    send_columns(1, 3)
    send_columns(1, 0)
    rep_copies = rep_second(rep_copies)
    forward(0)
    first_product(1, 1)
    rep_copies = rep_third(rep_copies)
    sent(0, 2, 3)
    send_rows(1, 0, 1, 0, KW // 2)
    send_rows(1, 1, 3, 0, KW // 2)
    product(1, 1)
    product(1, 3)
    rep_copies = rep_fourth(rep_copies)
    product(1, 0)
    for copy in loads[4:6]:
        copy.wait()
    turned = jnp.transpose(gains[...])
    current, gain = win[...], turned[:, 0:1]
    sent(0, 4, 5)
    reduce_rows(0)
    grad_gain = send_norm(0, current, gain)
    send_rows(1, 0, 1, 1, KW // 2)
    send_rows(1, 1, 3, 1, KW // 2)
    send_rows(1, 2, 1)
    send_rows(1, 3, 3)
    forward(1)
    current, gain, moments, gain_moments = update(
        0,
        current,
        gain,
        grad_gain,
        (m_one[...].astype(jnp.float32), m_two[...].astype(jnp.float32)),
        (turned[:, 1:2], turned[:, 2:3]),
    )
    for copy in rep_copies:
        copy.wait_recv()
    for copy in sends:
        copy.wait_send()
    sends.clear()
    reduce_rows(1)
    grad_gain = send_norm(1, current, gain)
    current, gain, _, _ = update(1, current, gain, grad_gain, moments, gain_moments)
    out_weight[...] = MIXING * current + (1.0 - MIXING) * merged[...]
    gain_total = gain_subs[0]
    for k in range(1, NL):
        gain_total = gain_total + gain_subs[k]
    anchor_row = gains[3:4, :]
    new_gain = outer_step(
        anchor_row, gains[4:5, :], anchor_row - gain_total / replicas
    )
    gain_row = jnp.transpose(jnp.broadcast_to(gain, (ROWS, 8)))
    out_gain[...] = MIXING * gain_row[0:1, :] + (1.0 - MIXING) * new_gain
    for copy in sends:
        copy.wait_send()


def window(*operands):
    anywhere = pl.BlockSpec(memory_space=pl.ANY)
    vmem = pl.BlockSpec(memory_space=pltpu.VMEM)
    dma = pltpu.SemaphoreType.DMA
    f32, bf16 = jnp.float32, jnp.bfloat16
    return pl.pallas_call(
        kernel,
        out_shape=(
            jax.ShapeDtypeStruct((ROWS, KW), f32),
            jax.ShapeDtypeStruct((1, ROWS), f32),
        ),
        in_specs=[anywhere] * len(operands),
        out_specs=(vmem, vmem),
        scratch_shapes=[
            pltpu.VMEM((INNER, TOK, D), bf16),
            pltpu.VMEM((INNER, TOK, KW), bf16),
            pltpu.VMEM((ROWS, KW), f32),
            pltpu.VMEM((ROWS, KW), bf16),
            pltpu.VMEM((ROWS, KW), bf16),
            pltpu.VMEM((INNER, NZ, NX * TOK, ROWS), bf16),
            pltpu.VMEM((INNER, NX * TOK, KW), bf16),
            pltpu.VMEM((INNER, ROWS, KW), f32),
            pltpu.VMEM((INNER, 2, HALF, KW), f32),
            pltpu.VMEM((INNER, 6, HALF, KW), bf16),
            pltpu.VMEM((INNER, 6, HALF, KW), bf16),
            pltpu.VMEM((INNER, NF, 1, 128), f32),
            pltpu.VMEM((NP, PART, KW), f32),
            pltpu.VMEM((PART, KW), f32),
            pltpu.VMEM((NL, SUB, KW), f32),
            pltpu.VMEM((ROWS, KW), f32),
            pltpu.VMEM((SUB, KW), f32),
            pltpu.VMEM((SUB, KW), f32),
            pltpu.VMEM((5, 1, ROWS), f32),
            pltpu.VMEM((8, ROWS), f32),
            pltpu.VMEM((NP, 1, ROWS), f32),
            pltpu.VMEM((NL, 1, ROWS), f32),
            dma((13 + INNER * NZ,)),
            dma((INNER, NZ, NX - 1)),
            dma((INNER, NZ, NX - 1)),
            dma((INNER, 2, NX - 1)),
            dma((INNER, 2, NX - 1)),
            dma((INNER, 8)),
            dma((INNER, 8)),
            dma((INNER, NF - 1)),
            dma((INNER, NF - 1)),
            dma((3, NP - 1)),
            dma((3, NP - 1)),
            dma((3, NL - 1)),
            dma((3, NL - 1)),
        ],
        compiler_params=pltpu.CompilerParams(
            collective_id=0, has_side_effects=True, vmem_limit_bytes=60 * 1024 * 1024
        ),
        cost_estimate=pl.CostEstimate(
            flops=4 * INNER * NX * TOK * NZ * ROWS * KW,
            bytes_accessed=8 * 1024 * 1024,
            transcendentals=0,
        ),
        name="inner_window",
    )(*operands)


def on_device(
    inputs,
    cotangent,
    weight,
    norm_gain,
    adam_first,
    adam_second,
    gain_first,
    gain_second,
    anchor_weight,
    anchor_gain,
    outer_weight,
    outer_gain,
):
    merged_weight, merged_gain = window(
        inputs,
        cotangent,
        weight[0],
        adam_first[0],
        adam_second[0],
        anchor_weight,
        outer_weight,
        norm_gain,
        gain_first,
        gain_second,
        anchor_gain[None],
        outer_gain[None],
    )
    return (merged_weight[None], merged_gain)


def solution(mesh):
    return jax.shard_map(
        on_device,
        mesh=mesh,
        in_specs=(
            P(None, ("rep", "fsdp"), None),
            P(None, ("rep", "fsdp"), None),
            P("rep", "fsdp", None),
            P("rep", "fsdp"),
            P("rep", "fsdp", None),
            P("rep", "fsdp", None),
            P("rep", "fsdp"),
            P("rep", "fsdp"),
            P("fsdp", None),
            P("fsdp"),
            P("fsdp", None),
            P("fsdp"),
        ),
        out_specs=(P("rep", "fsdp", None), P("rep", "fsdp")),
        check_vma=False,
    )
```

```python
import jax
import jax.numpy as jnp
from jax import lax
from jax.experimental import pallas as pl
from jax.experimental.pallas import tpu as pltpu
from jax.sharding import PartitionSpec as P

BETA_ONE = 0.9
BETA_TWO = 0.999
EPS_ADAM = 1e-08
RATE = 0.3
DECAY = 0.1
EPS_NORM = 1e-05
OUTER_RATE = 0.7
MOMENTUM = 0.9
MIXING = 0.5

INNER = 2
NX = 4
NZ = 4
NF = NX * NZ
TOK = 128
ROWS = 256
HALF = ROWS // 2
D = ROWS * NF
KW = 512
NP = 8
NL = 4
PART = ROWS // NP
SUB = PART // NL
PARTS = (4, 2)
ORDER = (2, 1, 3, 0)

MESH = pl.DeviceIdType.MESH


def flip(value, bits):
    if bits == 0:
        return value
    if bits == 1:
        return value + 1 - 2 * (value % 2)
    if bits == 2:
        return (value + 2) % 4
    return 3 - value


def adam_update(current, gradient, moment_one, moment_two, decay_rate):
    moment_one = BETA_ONE * moment_one + (1.0 - BETA_ONE) * gradient
    moment_two = BETA_TWO * moment_two + (1.0 - BETA_TWO) * gradient * gradient
    current = current - RATE * (
        moment_one / (jnp.sqrt(moment_two) + EPS_ADAM) + decay_rate * current
    )
    return (current, moment_one, moment_two)


def outer_step(anchor, momentum, mean_delta):
    velocity = MOMENTUM * momentum + mean_delta
    return anchor - OUTER_RATE * (mean_delta + MOMENTUM * velocity)


def kernel(
    inputs,
    cotangent,
    weight,
    adam_first,
    adam_second,
    anchor_weight,
    outer_weight,
    norm_gain,
    gain_first,
    gain_second,
    anchor_gain,
    outer_gain,
    out_weight,
    out_gain,
    xin,
    cin,
    win,
    m_one,
    m_two,
    columns,
    scaled,
    grads,
    keep,
    z_out,
    z_in,
    norms,
    parts,
    part_sum,
    subs,
    merged,
    anchor_rows,
    outer_rows,
    gain_in,
    gains,
    gain_parts,
    gain_subs,
    local_sem,
    x_send,
    x_recv,
    c_send,
    c_recv,
    z_send,
    z_recv,
    q_send,
    q_recv,
    p_send,
    p_recv,
    l_send,
    l_recv,
):
    replicas = NP * NL
    rep = lax.axis_index("rep")
    my_part = rep % NP
    my_plane = rep // NP
    me = lax.axis_index("fsdp")
    my_z = me // NX
    my_x = me % NX

    def at(z, x):
        return {"fsdp": z * NX + x}

    def in_plane(k):
        return {"rep": my_plane * NP + (my_part + k) % NP}

    def over_planes(k):
        return {"rep": (my_plane + k) % NL * NP + my_part}

    barrier = pltpu.get_barrier_semaphore()
    for j, i in ((0, 1), (0, 3), (0, 2), (1, 0), (3, 0)):
        pl.semaphore_signal(
            barrier, inc=1, device_id=at(flip(my_z, j), flip(my_x, i)), device_id_type=MESH
        )
    for k in range(1, NP):
        pl.semaphore_signal(barrier, inc=1, device_id=in_plane(k), device_id_type=MESH)
    for k in range(1, NL):
        pl.semaphore_signal(barrier, inc=1, device_id=over_planes(k), device_id_type=MESH)

    def part_of(part):
        return pl.ds(pl.multiple_of(part * PART, PART), PART)

    sub_rows = pl.ds(pl.multiple_of(my_part * PART + my_plane * SUB, SUB), SUB)

    loads = []
    for place, (source, target) in enumerate(
        (
            (inputs.at[0], xin.at[0]),
            (cotangent, cin),
            (inputs.at[1], xin.at[1]),
            (weight, win),
            (adam_first, m_one),
            (adam_second, m_two),
            (anchor_weight.at[sub_rows], anchor_rows),
            (outer_weight.at[sub_rows], outer_rows),
            (norm_gain, gain_in.at[0]),
            (gain_first, gain_in.at[1]),
            (gain_second, gain_in.at[2]),
            (anchor_gain, gain_in.at[3]),
            (outer_gain, gain_in.at[4]),
        )
    ):
        copy = pltpu.make_async_copy(source, target, local_sem.at[place])
        copy.start()
        loads.append(copy)

    def column(j, i):
        owner = flip(my_z, j) * NX + flip(my_x, i)
        return pl.ds(pl.multiple_of(owner * ROWS, ROWS), ROWS)

    own_copies = {}
    place = len(loads)
    for s in range(INNER):
        for j in ORDER:
            copy = pltpu.make_async_copy(
                inputs.at[s, :, column(j, 0)],
                columns.at[s, j, pl.ds(0, TOK)],
                local_sem.at[place],
            )
            copy.start()
            own_copies[s, j] = copy
            place += 1

    sends = []

    def send(source, target, send_sem, recv_sem, device):
        copy = pltpu.make_async_remote_copy(
            src_ref=source,
            dst_ref=target,
            send_sem=send_sem,
            recv_sem=recv_sem,
            device_id=device,
            device_id_type=MESH,
        )
        copy.start()
        sends.append(copy)
        return copy

    x_copies = {}
    c_copies = {}
    z_copies = {}
    q_copies = {}

    def send_columns(s, j):
        x_copies[s, j] = [
            send(
                inputs.at[s, :, column(j, i)],
                columns.at[s, j, pl.ds(i * TOK, TOK)],
                x_send.at[s, j, i - 1],
                x_recv.at[s, j, i - 1],
                at(my_z, flip(my_x, i)),
            )
            for i in (1, 3, 2)
        ]

    def scale(s):
        values = xin[s].astype(jnp.float32)
        mean = jnp.mean(values * values, axis=-1, keepdims=True)
        scale = lax.rsqrt(mean + EPS_NORM)
        scaled[s, pl.ds(0, TOK), :] = (cin[s].astype(jnp.float32) * scale).astype(
            jnp.bfloat16
        )

    def send_scaled(s, part, width):
        columns_of = pl.ds(part * width, width)
        c_copies[s, part] = [
            send(
                scaled.at[s, pl.ds(0, TOK), columns_of],
                scaled.at[s, pl.ds(i * TOK, TOK), columns_of],
                c_send.at[s, part, i - 1],
                c_recv.at[s, part, i - 1],
                at(my_z, flip(my_x, i)),
            )
            for i in (1, 3, 2)
        ]

    def send_rows(s, slot, j, part=0, width=KW):
        columns_of = pl.ds(part * width, width)
        sem = slot if part == 0 else 4 + 2 * part + slot
        z_copies[s, sem] = send(
            z_out.at[s, slot, :, columns_of],
            z_in.at[s, slot, :, columns_of],
            z_send.at[s, sem],
            z_recv.at[s, sem],
            at(flip(my_z, j), my_x),
        )

    def sent(s, *slots):
        for slot in slots:
            copy = z_copies[s, slot]
            copy.wait_send()
            sends[:] = [other for other in sends if other is not copy]


    def exchange(stage, sems, count, source, target, device):
        return [
            send(
                source(k),
                target(k),
                sems[0].at[stage, k - 1],
                sems[1].at[stage, k - 1],
                device(k),
            )
            for k in range(1, count)
        ]

    planes = (p_send, p_recv), NP
    levels = (l_send, l_recv), NL

    def rep_start():
        return exchange(
            0,
            *planes,
            lambda k: weight.at[part_of((my_part + k) % NP)],
            lambda k: parts.at[k],
            in_plane,
        ) + exchange(
            1, *planes, lambda k: gain_in.at[0], lambda k: gain_parts.at[k], in_plane
        )

    def rep_second(copies):
        for copy in copies:
            copy.wait_recv()
        loads[3].wait()
        total = win[part_of(my_part), :]
        for k in range(1, NP):
            total = total + parts[k]
        part_sum[...] = total
        gain_total = gain_in[0]
        for k in range(1, NP):
            gain_total = gain_total + gain_parts[k]
        gain_subs[0] = gain_total
        return exchange(
            0,
            *levels,
            lambda k: part_sum.at[
                pl.ds(pl.multiple_of((my_plane + k) % NL * SUB, SUB), SUB)
            ],
            lambda k: subs.at[k],
            over_planes,
        ) + exchange(
            1, *levels, lambda k: gain_subs.at[0], lambda k: gain_subs.at[k], over_planes
        )

    def rep_third(copies):
        for copy in copies:
            copy.wait_recv()
        total = part_sum[pl.ds(pl.multiple_of(my_plane * SUB, SUB), SUB), :]
        for k in range(1, NL):
            total = total + subs[k]
        loads[6].wait()
        loads[7].wait()
        anchor = anchor_rows[...]
        merged[sub_rows, :] = outer_step(
            anchor, outer_rows[...], anchor - total / replicas
        )
        return exchange(
            2,
            *levels,
            lambda k: merged.at[sub_rows],
            lambda k: merged.at[sub_rows],
            over_planes,
        )

    def rep_fourth(copies):
        for copy in copies:
            copy.wait_recv()
        return exchange(
            2,
            *planes,
            lambda k: merged.at[part_of(my_part)],
            lambda k: merged.at[part_of(my_part)],
            in_plane,
        )

    low = pl.ds(0, HALF)
    high = pl.ds(HALF, HALF)

    def multiply(s, j, columns_of):
        return lax.dot_general(
            columns[s, j],
            scaled[s, :, columns_of],
            (((0,), (0,)), ((), ())),
            preferred_element_type=jnp.float32,
        )

    def arrived(s, j, part=None):
        if part in (None, 0):
            own_copies[s, j].wait()
            for copy in x_copies[s, j]:
                copy.wait_recv()
        if part is not None:
            for copy in c_copies[s, part]:
                copy.wait_recv()

    def first_product(s, parts_of):
        width = KW // parts_of
        for part in range(parts_of):
            arrived(s, 2, part)
            columns_of = pl.ds(part * width, width)
            block = multiply(s, 2, columns_of)
            z_out[s, 0, :, columns_of] = block[:HALF].astype(jnp.bfloat16)
            z_out[s, 1, :, columns_of] = block[HALF:].astype(jnp.bfloat16)
            if s == 0:
                send_rows(s, 0, 1, part, width)
                send_rows(s, 1, 3, part, width)

    def product(s, j):
        arrived(s, j)
        block = multiply(s, j, pl.ds(0, KW))
        if j == 1:
            z_out[s, 2] = block[:HALF].astype(jnp.bfloat16)
            keep[s, 1] = block[HALF:]
        elif j == 3:
            z_out[s, 3] = block[HALF:].astype(jnp.bfloat16)
            keep[s, 0] = block[:HALF]
        else:
            grads[s] = block

    def forward(s):
        for slot, target, j in ((0, 4, 3), (1, 5, 1)):
            z_copies[s, slot].wait_recv()
            for part in range(1, PARTS[s]):
                z_copies[s, 4 + 2 * part + slot].wait_recv()
            total = keep[s, slot] + z_in[s, slot].astype(jnp.float32)
            z_out[s, target] = total.astype(jnp.bfloat16)
            send_rows(s, target, j)

    def reduce_rows(s):
        for slot in (2, 3, 4, 5):
            z_copies[s, slot].wait_recv()
        grads[s, low] = grads[s, low] + (
            z_in[s, 2].astype(jnp.float32) + z_in[s, 4].astype(jnp.float32)
        )
        grads[s, high] = grads[s, high] + (
            z_in[s, 3].astype(jnp.float32) + z_in[s, 5].astype(jnp.float32)
        )

    def send_norm(s, current, gain):
        product_sum = grads[s]
        low_weight = current.astype(jnp.bfloat16).astype(jnp.float32)
        grad_gain = jnp.sum(product_sum * low_weight, axis=1, keepdims=True)
        grad_weight = product_sum * gain
        squares = grad_weight * grad_weight
        folded = squares[:, 0:128] + squares[:, 128:256] + squares[:, 256:384] + squares[:, 384:512]
        lane = lax.broadcasted_iota(jnp.int32, (ROWS, 128), 1)
        folded = folded + jnp.where(lane == 0, grad_gain * grad_gain, 0.0)
        norms[s, 0] = jnp.sum(folded, axis=0, keepdims=True)
        q_copies[s] = [
            send(
                norms.at[s, 0],
                norms.at[s, k],
                q_send.at[s, k - 1],
                q_recv.at[s, k - 1],
                {"fsdp": (me + k) % NF},
            )
            for k in range(1, NF)
        ]
        return grad_gain

    def update(s, current, gain, grad_gain, moments, gain_moments):
        for copy in q_copies[s]:
            copy.wait_recv()
        total = jnp.sum(jnp.sum(norms[s], axis=0), keepdims=True)
        factor = jnp.minimum(1.0, 1.0 / (jnp.sqrt(total) + 1e-06))
        current, one, two = adam_update(
            current, factor * (grads[s] * gain), moments[0], moments[1], DECAY
        )
        gain, gain_one, gain_two = adam_update(
            gain, factor * grad_gain, gain_moments[0], gain_moments[1], 0.0
        )
        return current, gain, (one, two), (gain_one, gain_two)

    pl.semaphore_wait(barrier, 5 + NP + NL - 2)

    send_columns(0, 2)
    for copy in loads[:2]:
        copy.wait()
    scale(0)
    for part in range(PARTS[0]):
        send_scaled(0, part, KW // PARTS[0])
    for copy in loads[8:]:
        copy.wait()
    gains[...] = jnp.concatenate(
        [gain_in[k] for k in range(5)] + [jnp.zeros((3, ROWS), jnp.float32)], axis=0
    )
    rep_copies = rep_start()
    send_columns(0, 1)
    first_product(0, PARTS[0])
    send_columns(0, 3)
    send_columns(0, 0)
    product(0, 1)
    send_rows(0, 2, 1)
    loads[2].wait()
    scale(1)
    send_scaled(1, 0, KW)
    send_columns(1, 2)
    product(0, 3)
    send_rows(0, 3, 3)
    product(0, 0)
    send_columns(1, 1)
    send_columns(1, 3)
    send_columns(1, 0)
    rep_copies = rep_second(rep_copies)
    forward(0)
    first_product(1, 1)
    rep_copies = rep_third(rep_copies)
    sent(0, 2, 3)
    send_rows(1, 0, 1, 0, KW // 2)
    send_rows(1, 1, 3, 0, KW // 2)
    product(1, 1)
    product(1, 3)
    rep_copies = rep_fourth(rep_copies)
    product(1, 0)
    for copy in loads[4:6]:
        copy.wait()
    turned = jnp.transpose(gains[...])
    current, gain = win[...], turned[:, 0:1]
    sent(0, 4, 5)
    reduce_rows(0)
    grad_gain = send_norm(0, current, gain)
    send_rows(1, 0, 1, 1, KW // 2)
    send_rows(1, 1, 3, 1, KW // 2)
    send_rows(1, 2, 1)
    send_rows(1, 3, 3)
    forward(1)
    current, gain, moments, gain_moments = update(
        0,
        current,
        gain,
        grad_gain,
        (m_one[...].astype(jnp.float32), m_two[...].astype(jnp.float32)),
        (turned[:, 1:2], turned[:, 2:3]),
    )
    for copy in rep_copies:
        copy.wait_recv()
    for copy in sends:
        copy.wait_send()
    sends.clear()
    reduce_rows(1)
    grad_gain = send_norm(1, current, gain)
    current, gain, _, _ = update(1, current, gain, grad_gain, moments, gain_moments)
    out_weight[...] = MIXING * current + (1.0 - MIXING) * merged[...]
    gain_total = gain_subs[0]
    for k in range(1, NL):
        gain_total = gain_total + gain_subs[k]
    anchor_row = gains[3:4, :]
    new_gain = outer_step(
        anchor_row, gains[4:5, :], anchor_row - gain_total / replicas
    )
    gain_row = jnp.transpose(jnp.broadcast_to(gain, (ROWS, 8)))
    out_gain[...] = MIXING * gain_row[0:1, :] + (1.0 - MIXING) * new_gain
    for copy in sends:
        copy.wait_send()


def window(*operands):
    anywhere = pl.BlockSpec(memory_space=pl.ANY)
    vmem = pl.BlockSpec(memory_space=pltpu.VMEM)
    dma = pltpu.SemaphoreType.DMA
    f32, bf16 = jnp.float32, jnp.bfloat16
    return pl.pallas_call(
        kernel,
        out_shape=(
            jax.ShapeDtypeStruct((ROWS, KW), f32),
            jax.ShapeDtypeStruct((1, ROWS), f32),
        ),
        in_specs=[anywhere] * len(operands),
        out_specs=(vmem, vmem),
        scratch_shapes=[
            pltpu.VMEM((INNER, TOK, D), bf16),
            pltpu.VMEM((INNER, TOK, KW), bf16),
            pltpu.VMEM((ROWS, KW), f32),
            pltpu.VMEM((ROWS, KW), bf16),
            pltpu.VMEM((ROWS, KW), bf16),
            pltpu.VMEM((INNER, NZ, NX * TOK, ROWS), bf16),
            pltpu.VMEM((INNER, NX * TOK, KW), bf16),
            pltpu.VMEM((INNER, ROWS, KW), f32),
            pltpu.VMEM((INNER, 2, HALF, KW), f32),
            pltpu.VMEM((INNER, 6, HALF, KW), bf16),
            pltpu.VMEM((INNER, 6, HALF, KW), bf16),
            pltpu.VMEM((INNER, NF, 1, 128), f32),
            pltpu.VMEM((NP, PART, KW), f32),
            pltpu.VMEM((PART, KW), f32),
            pltpu.VMEM((NL, SUB, KW), f32),
            pltpu.VMEM((ROWS, KW), f32),
            pltpu.VMEM((SUB, KW), f32),
            pltpu.VMEM((SUB, KW), f32),
            pltpu.VMEM((5, 1, ROWS), f32),
            pltpu.VMEM((8, ROWS), f32),
            pltpu.VMEM((NP, 1, ROWS), f32),
            pltpu.VMEM((NL, 1, ROWS), f32),
            dma((13 + INNER * NZ,)),
            dma((INNER, NZ, NX - 1)),
            dma((INNER, NZ, NX - 1)),
            dma((INNER, PARTS[0], NX - 1)),
            dma((INNER, PARTS[0], NX - 1)),
            dma((INNER, 4 + 2 * PARTS[0])),
            dma((INNER, 4 + 2 * PARTS[0])),
            dma((INNER, NF - 1)),
            dma((INNER, NF - 1)),
            dma((3, NP - 1)),
            dma((3, NP - 1)),
            dma((3, NL - 1)),
            dma((3, NL - 1)),
        ],
        compiler_params=pltpu.CompilerParams(
            collective_id=0, has_side_effects=True, vmem_limit_bytes=60 * 1024 * 1024
        ),
        cost_estimate=pl.CostEstimate(
            flops=4 * INNER * NX * TOK * NZ * ROWS * KW,
            bytes_accessed=8 * 1024 * 1024,
            transcendentals=0,
        ),
        name="inner_window",
    )(*operands)


def on_device(
    inputs,
    cotangent,
    weight,
    norm_gain,
    adam_first,
    adam_second,
    gain_first,
    gain_second,
    anchor_weight,
    anchor_gain,
    outer_weight,
    outer_gain,
):
    merged_weight, merged_gain = window(
        inputs,
        cotangent,
        weight[0],
        adam_first[0],
        adam_second[0],
        anchor_weight,
        outer_weight,
        norm_gain,
        gain_first,
        gain_second,
        anchor_gain[None],
        outer_gain[None],
    )
    return (merged_weight[None], merged_gain)


def solution(mesh):
    return jax.shard_map(
        on_device,
        mesh=mesh,
        in_specs=(
            P(None, ("rep", "fsdp"), None),
            P(None, ("rep", "fsdp"), None),
            P("rep", "fsdp", None),
            P("rep", "fsdp"),
            P("rep", "fsdp", None),
            P("rep", "fsdp", None),
            P("rep", "fsdp"),
            P("rep", "fsdp"),
            P("fsdp", None),
            P("fsdp"),
            P("fsdp", None),
            P("fsdp"),
        ),
        out_specs=(P("rep", "fsdp", None), P("rep", "fsdp")),
        check_vma=False,
    )
```

```python
import jax
import jax.numpy as jnp
from jax import lax
from jax.experimental import pallas as pl
from jax.experimental.pallas import tpu as pltpu
from jax.sharding import PartitionSpec as P

BETA_ONE = 0.9
BETA_TWO = 0.999
EPS_ADAM = 1e-08
RATE = 0.3
DECAY = 0.1
EPS_NORM = 1e-05
OUTER_RATE = 0.7
MOMENTUM = 0.9
MIXING = 0.5

INNER = 2
NX = 4
NZ = 4
NF = NX * NZ
TOK = 128
ROWS = 256
HALF = ROWS // 2
D = ROWS * NF
KW = 512
NP = 8
NL = 4
PART = ROWS // NP
SUB = PART // NL
PARTS = (4, 2)
ORDER = (2, 1, 3, 0)

FAR_FIRST = [(j, i) for j in (2, 1, 3, 0) for i in (2, 1, 3, 0) if i + j > 0]

MESH = pl.DeviceIdType.MESH


def flip(value, bits):
    if bits == 0:
        return value
    if bits == 1:
        return value + 1 - 2 * (value % 2)
    if bits == 2:
        return (value + 2) % 4
    return 3 - value


def adam_update(current, gradient, moment_one, moment_two, decay_rate):
    moment_one = BETA_ONE * moment_one + (1.0 - BETA_ONE) * gradient
    moment_two = BETA_TWO * moment_two + (1.0 - BETA_TWO) * gradient * gradient
    current = current - RATE * (
        moment_one / (jnp.sqrt(moment_two) + EPS_ADAM) + decay_rate * current
    )
    return (current, moment_one, moment_two)


def outer_step(anchor, momentum, mean_delta):
    velocity = MOMENTUM * momentum + mean_delta
    return anchor - OUTER_RATE * (mean_delta + MOMENTUM * velocity)


def kernel(
    inputs,
    cotangent,
    weight,
    adam_first,
    adam_second,
    anchor_weight,
    outer_weight,
    norm_gain,
    gain_first,
    gain_second,
    anchor_gain,
    outer_gain,
    out_weight,
    out_gain,
    xin,
    cin,
    win,
    m_one,
    m_two,
    columns,
    scaled,
    grads,
    keep,
    z_out,
    z_in,
    norms,
    parts,
    part_sum,
    subs,
    merged,
    anchor_rows,
    outer_rows,
    gain_in,
    gains,
    gain_parts,
    gain_subs,
    local_sem,
    x_send,
    x_recv,
    c_send,
    c_recv,
    z_send,
    z_recv,
    q_send,
    q_recv,
    p_send,
    p_recv,
    l_send,
    l_recv,
):
    replicas = NP * NL
    rep = lax.axis_index("rep")
    my_part = rep % NP
    my_plane = rep // NP
    me = lax.axis_index("fsdp")
    my_z = me // NX
    my_x = me % NX

    def at(z, x):
        return {"fsdp": z * NX + x}

    def in_plane(k):
        return {"rep": my_plane * NP + (my_part + k) % NP}

    def over_planes(k):
        return {"rep": (my_plane + k) % NL * NP + my_part}

    barrier = pltpu.get_barrier_semaphore()
    for j, i in ((0, 1), (0, 3), (0, 2), (1, 0), (3, 0)):
        pl.semaphore_signal(
            barrier, inc=1, device_id=at(flip(my_z, j), flip(my_x, i)), device_id_type=MESH
        )
    for k in range(1, NP):
        pl.semaphore_signal(barrier, inc=1, device_id=in_plane(k), device_id_type=MESH)
    for k in range(1, NL):
        pl.semaphore_signal(barrier, inc=1, device_id=over_planes(k), device_id_type=MESH)

    def part_of(part):
        return pl.ds(pl.multiple_of(part * PART, PART), PART)

    sub_rows = pl.ds(pl.multiple_of(my_part * PART + my_plane * SUB, SUB), SUB)

    loads = []
    for place, (source, target) in enumerate(
        (
            (inputs.at[0], xin.at[0]),
            (cotangent, cin),
            (inputs.at[1], xin.at[1]),
            (weight, win),
            (adam_first, m_one),
            (adam_second, m_two),
            (anchor_weight.at[sub_rows], anchor_rows),
            (outer_weight.at[sub_rows], outer_rows),
            (norm_gain, gain_in.at[0]),
            (gain_first, gain_in.at[1]),
            (gain_second, gain_in.at[2]),
            (anchor_gain, gain_in.at[3]),
            (outer_gain, gain_in.at[4]),
        )
    ):
        copy = pltpu.make_async_copy(source, target, local_sem.at[place])
        copy.start()
        loads.append(copy)

    def column(j, i):
        owner = flip(my_z, j) * NX + flip(my_x, i)
        return pl.ds(pl.multiple_of(owner * ROWS, ROWS), ROWS)

    own_copies = {}
    place = len(loads)
    for s in range(INNER):
        for j in ORDER:
            copy = pltpu.make_async_copy(
                inputs.at[s, :, column(j, 0)],
                columns.at[s, j, pl.ds(0, TOK)],
                local_sem.at[place],
            )
            copy.start()
            own_copies[s, j] = copy
            place += 1

    sends = []

    def send(source, target, send_sem, recv_sem, device):
        copy = pltpu.make_async_remote_copy(
            src_ref=source,
            dst_ref=target,
            send_sem=send_sem,
            recv_sem=recv_sem,
            device_id=device,
            device_id_type=MESH,
        )
        copy.start()
        sends.append(copy)
        return copy

    x_copies = {}
    c_copies = {}
    z_copies = {}
    q_copies = {}

    def send_columns(s, j):
        x_copies[s, j] = [
            send(
                inputs.at[s, :, column(j, i)],
                columns.at[s, j, pl.ds(i * TOK, TOK)],
                x_send.at[s, j, i - 1],
                x_recv.at[s, j, i - 1],
                at(my_z, flip(my_x, i)),
            )
            for i in (1, 3, 2)
        ]

    def scale(s):
        values = xin[s].astype(jnp.float32)
        mean = jnp.mean(values * values, axis=-1, keepdims=True)
        scale = lax.rsqrt(mean + EPS_NORM)
        scaled[s, pl.ds(0, TOK), :] = (cin[s].astype(jnp.float32) * scale).astype(
            jnp.bfloat16
        )

    def send_scaled(s, part, width):
        columns_of = pl.ds(part * width, width)
        c_copies[s, part] = [
            send(
                scaled.at[s, pl.ds(0, TOK), columns_of],
                scaled.at[s, pl.ds(i * TOK, TOK), columns_of],
                c_send.at[s, part, i - 1],
                c_recv.at[s, part, i - 1],
                at(my_z, flip(my_x, i)),
            )
            for i in (1, 3, 2)
        ]

    def send_rows(s, slot, j, part=0, width=KW):
        columns_of = pl.ds(part * width, width)
        sem = slot if part == 0 else 4 + 2 * part + slot
        z_copies[s, sem] = send(
            z_out.at[s, slot, :, columns_of],
            z_in.at[s, slot, :, columns_of],
            z_send.at[s, sem],
            z_recv.at[s, sem],
            at(flip(my_z, j), my_x),
        )

    def sent(s, *slots):
        for slot in slots:
            copy = z_copies[s, slot]
            copy.wait_send()
            sends[:] = [other for other in sends if other is not copy]


    def exchange(stage, sems, count, source, target, device):
        return [
            send(
                source(k),
                target(k),
                sems[0].at[stage, k - 1],
                sems[1].at[stage, k - 1],
                device(k),
            )
            for k in range(1, count)
        ]

    planes = (p_send, p_recv), NP
    levels = (l_send, l_recv), NL

    def rep_start():
        return exchange(
            0,
            *planes,
            lambda k: weight.at[part_of((my_part + k) % NP)],
            lambda k: parts.at[k],
            in_plane,
        ) + exchange(
            1, *planes, lambda k: gain_in.at[0], lambda k: gain_parts.at[k], in_plane
        )

    def rep_second(copies):
        for copy in copies:
            copy.wait_recv()
        loads[3].wait()
        total = win[part_of(my_part), :]
        for k in range(1, NP):
            total = total + parts[k]
        part_sum[...] = total
        gain_total = gain_in[0]
        for k in range(1, NP):
            gain_total = gain_total + gain_parts[k]
        gain_subs[0] = gain_total
        return exchange(
            0,
            *levels,
            lambda k: part_sum.at[
                pl.ds(pl.multiple_of((my_plane + k) % NL * SUB, SUB), SUB)
            ],
            lambda k: subs.at[k],
            over_planes,
        ) + exchange(
            1, *levels, lambda k: gain_subs.at[0], lambda k: gain_subs.at[k], over_planes
        )

    def rep_third(copies):
        for copy in copies:
            copy.wait_recv()
        total = part_sum[pl.ds(pl.multiple_of(my_plane * SUB, SUB), SUB), :]
        for k in range(1, NL):
            total = total + subs[k]
        loads[6].wait()
        loads[7].wait()
        anchor = anchor_rows[...]
        merged[sub_rows, :] = outer_step(
            anchor, outer_rows[...], anchor - total / replicas
        )
        return exchange(
            2,
            *levels,
            lambda k: merged.at[sub_rows],
            lambda k: merged.at[sub_rows],
            over_planes,
        )

    def rep_fourth(copies):
        for copy in copies:
            copy.wait_recv()
        return exchange(
            2,
            *planes,
            lambda k: merged.at[part_of(my_part)],
            lambda k: merged.at[part_of(my_part)],
            in_plane,
        )

    low = pl.ds(0, HALF)
    high = pl.ds(HALF, HALF)

    def multiply(s, j, columns_of):
        return lax.dot_general(
            columns[s, j],
            scaled[s, :, columns_of],
            (((0,), (0,)), ((), ())),
            preferred_element_type=jnp.float32,
        )

    def arrived(s, j, part=None):
        if part in (None, 0):
            own_copies[s, j].wait()
            for copy in x_copies[s, j]:
                copy.wait_recv()
        if part is not None:
            for copy in c_copies[s, part]:
                copy.wait_recv()

    def first_product(s, parts_of):
        width = KW // parts_of
        for part in range(parts_of):
            arrived(s, 2, part)
            columns_of = pl.ds(part * width, width)
            block = multiply(s, 2, columns_of)
            z_out[s, 0, :, columns_of] = block[:HALF].astype(jnp.bfloat16)
            z_out[s, 1, :, columns_of] = block[HALF:].astype(jnp.bfloat16)
            if s == 0:
                send_rows(s, 0, 1, part, width)
                send_rows(s, 1, 3, part, width)

    def product(s, j):
        arrived(s, j)
        block = multiply(s, j, pl.ds(0, KW))
        if j == 1:
            z_out[s, 2] = block[:HALF].astype(jnp.bfloat16)
            keep[s, 1] = block[HALF:]
        elif j == 3:
            z_out[s, 3] = block[HALF:].astype(jnp.bfloat16)
            keep[s, 0] = block[:HALF]
        else:
            grads[s] = block

    def forward(s):
        for slot, target, j in ((0, 4, 3), (1, 5, 1)):
            z_copies[s, slot].wait_recv()
            for part in range(1, PARTS[s]):
                z_copies[s, 4 + 2 * part + slot].wait_recv()
            total = keep[s, slot] + z_in[s, slot].astype(jnp.float32)
            z_out[s, target] = total.astype(jnp.bfloat16)
            send_rows(s, target, j)

    def reduce_rows(s):
        for slot in (2, 3, 4, 5):
            z_copies[s, slot].wait_recv()
        grads[s, low] = grads[s, low] + (
            z_in[s, 2].astype(jnp.float32) + z_in[s, 4].astype(jnp.float32)
        )
        grads[s, high] = grads[s, high] + (
            z_in[s, 3].astype(jnp.float32) + z_in[s, 5].astype(jnp.float32)
        )

    def send_norm(s, current, gain):
        product_sum = grads[s]
        low_weight = current.astype(jnp.bfloat16).astype(jnp.float32)
        grad_gain = jnp.sum(product_sum * low_weight, axis=1, keepdims=True)
        grad_weight = product_sum * gain
        squares = grad_weight * grad_weight
        folded = squares[:, 0:128] + squares[:, 128:256] + squares[:, 256:384] + squares[:, 384:512]
        lane = lax.broadcasted_iota(jnp.int32, (ROWS, 128), 1)
        folded = folded + jnp.where(lane == 0, grad_gain * grad_gain, 0.0)
        norms[s, 0] = jnp.sum(folded, axis=0, keepdims=True)
        q_copies[s] = [
            send(
                norms.at[s, 0],
                norms.at[s, k],
                q_send.at[s, k - 1],
                q_recv.at[s, k - 1],
                at(flip(my_z, j), flip(my_x, i)),
            )
            for k, (j, i) in enumerate(FAR_FIRST, 1)
        ]
        return grad_gain

    def update(s, current, gain, grad_gain, moments, gain_moments):
        for copy in q_copies[s]:
            copy.wait_recv()
        total = jnp.sum(jnp.sum(norms[s], axis=0), keepdims=True)
        factor = jnp.minimum(1.0, 1.0 / (jnp.sqrt(total) + 1e-06))
        current, one, two = adam_update(
            current, factor * (grads[s] * gain), moments[0], moments[1], DECAY
        )
        gain, gain_one, gain_two = adam_update(
            gain, factor * grad_gain, gain_moments[0], gain_moments[1], 0.0
        )
        return current, gain, (one, two), (gain_one, gain_two)

    pl.semaphore_wait(barrier, 5 + NP + NL - 2)

    send_columns(0, 2)
    for copy in loads[:2]:
        copy.wait()
    scale(0)
    for part in range(PARTS[0]):
        send_scaled(0, part, KW // PARTS[0])
    for copy in loads[8:]:
        copy.wait()
    gains[...] = jnp.concatenate(
        [gain_in[k] for k in range(5)] + [jnp.zeros((3, ROWS), jnp.float32)], axis=0
    )
    rep_copies = rep_start()
    send_columns(0, 1)
    first_product(0, PARTS[0])
    send_columns(0, 3)
    send_columns(0, 0)
    product(0, 1)
    send_rows(0, 2, 1)
    loads[2].wait()
    scale(1)
    send_scaled(1, 0, KW)
    send_columns(1, 2)
    product(0, 3)
    send_rows(0, 3, 3)
    product(0, 0)
    send_columns(1, 1)
    send_columns(1, 3)
    send_columns(1, 0)
    rep_copies = rep_second(rep_copies)
    forward(0)
    first_product(1, 1)
    sent(0, 2, 3)
    send_rows(1, 0, 1, 0, KW // 2)
    send_rows(1, 1, 3, 0, KW // 2)
    rep_copies = rep_third(rep_copies)
    product(1, 1)
    product(1, 3)
    product(1, 0)
    for copy in loads[4:6]:
        copy.wait()
    turned = jnp.transpose(gains[...])
    current, gain = win[...], turned[:, 0:1]
    sent(0, 4, 5)
    reduce_rows(0)
    grad_gain = send_norm(0, current, gain)
    send_rows(1, 0, 1, 1, KW // 2)
    send_rows(1, 1, 3, 1, KW // 2)
    send_rows(1, 2, 1)
    send_rows(1, 3, 3)
    forward(1)
    rep_copies = rep_fourth(rep_copies)
    current, gain, moments, gain_moments = update(
        0,
        current,
        gain,
        grad_gain,
        (m_one[...].astype(jnp.float32), m_two[...].astype(jnp.float32)),
        (turned[:, 1:2], turned[:, 2:3]),
    )
    for copy in rep_copies:
        copy.wait_recv()
    for copy in sends:
        copy.wait_send()
    sends.clear()
    reduce_rows(1)
    grad_gain = send_norm(1, current, gain)
    current, gain, _, _ = update(1, current, gain, grad_gain, moments, gain_moments)
    out_weight[...] = MIXING * current + (1.0 - MIXING) * merged[...]
    gain_total = gain_subs[0]
    for k in range(1, NL):
        gain_total = gain_total + gain_subs[k]
    anchor_row = gains[3:4, :]
    new_gain = outer_step(
        anchor_row, gains[4:5, :], anchor_row - gain_total / replicas
    )
    gain_row = jnp.transpose(jnp.broadcast_to(gain, (ROWS, 8)))
    out_gain[...] = MIXING * gain_row[0:1, :] + (1.0 - MIXING) * new_gain
    for copy in sends:
        copy.wait_send()


def window(*operands):
    anywhere = pl.BlockSpec(memory_space=pl.ANY)
    vmem = pl.BlockSpec(memory_space=pltpu.VMEM)
    dma = pltpu.SemaphoreType.DMA
    f32, bf16 = jnp.float32, jnp.bfloat16
    return pl.pallas_call(
        kernel,
        out_shape=(
            jax.ShapeDtypeStruct((ROWS, KW), f32),
            jax.ShapeDtypeStruct((1, ROWS), f32),
        ),
        in_specs=[anywhere] * len(operands),
        out_specs=(vmem, vmem),
        scratch_shapes=[
            pltpu.VMEM((INNER, TOK, D), bf16),
            pltpu.VMEM((INNER, TOK, KW), bf16),
            pltpu.VMEM((ROWS, KW), f32),
            pltpu.VMEM((ROWS, KW), bf16),
            pltpu.VMEM((ROWS, KW), bf16),
            pltpu.VMEM((INNER, NZ, NX * TOK, ROWS), bf16),
            pltpu.VMEM((INNER, NX * TOK, KW), bf16),
            pltpu.VMEM((INNER, ROWS, KW), f32),
            pltpu.VMEM((INNER, 2, HALF, KW), f32),
            pltpu.VMEM((INNER, 6, HALF, KW), bf16),
            pltpu.VMEM((INNER, 6, HALF, KW), bf16),
            pltpu.VMEM((INNER, NF, 1, 128), f32),
            pltpu.VMEM((NP, PART, KW), f32),
            pltpu.VMEM((PART, KW), f32),
            pltpu.VMEM((NL, SUB, KW), f32),
            pltpu.VMEM((ROWS, KW), f32),
            pltpu.VMEM((SUB, KW), f32),
            pltpu.VMEM((SUB, KW), f32),
            pltpu.VMEM((5, 1, ROWS), f32),
            pltpu.VMEM((8, ROWS), f32),
            pltpu.VMEM((NP, 1, ROWS), f32),
            pltpu.VMEM((NL, 1, ROWS), f32),
            dma((13 + INNER * NZ,)),
            dma((INNER, NZ, NX - 1)),
            dma((INNER, NZ, NX - 1)),
            dma((INNER, PARTS[0], NX - 1)),
            dma((INNER, PARTS[0], NX - 1)),
            dma((INNER, 4 + 2 * PARTS[0])),
            dma((INNER, 4 + 2 * PARTS[0])),
            dma((INNER, NF - 1)),
            dma((INNER, NF - 1)),
            dma((3, NP - 1)),
            dma((3, NP - 1)),
            dma((3, NL - 1)),
            dma((3, NL - 1)),
        ],
        compiler_params=pltpu.CompilerParams(
            collective_id=0, has_side_effects=True, vmem_limit_bytes=60 * 1024 * 1024
        ),
        cost_estimate=pl.CostEstimate(
            flops=4 * INNER * NX * TOK * NZ * ROWS * KW,
            bytes_accessed=8 * 1024 * 1024,
            transcendentals=0,
        ),
        name="inner_window",
    )(*operands)


def on_device(
    inputs,
    cotangent,
    weight,
    norm_gain,
    adam_first,
    adam_second,
    gain_first,
    gain_second,
    anchor_weight,
    anchor_gain,
    outer_weight,
    outer_gain,
):
    merged_weight, merged_gain = window(
        inputs,
        cotangent,
        weight[0],
        adam_first[0],
        adam_second[0],
        anchor_weight,
        outer_weight,
        norm_gain,
        gain_first,
        gain_second,
        anchor_gain[None],
        outer_gain[None],
    )
    return (merged_weight[None], merged_gain)


def solution(mesh):
    return jax.shard_map(
        on_device,
        mesh=mesh,
        in_specs=(
            P(None, ("rep", "fsdp"), None),
            P(None, ("rep", "fsdp"), None),
            P("rep", "fsdp", None),
            P("rep", "fsdp"),
            P("rep", "fsdp", None),
            P("rep", "fsdp", None),
            P("rep", "fsdp"),
            P("rep", "fsdp"),
            P("fsdp", None),
            P("fsdp"),
            P("fsdp", None),
            P("fsdp"),
        ),
        out_specs=(P("rep", "fsdp", None), P("rep", "fsdp")),
        check_vma=False,
    )
```

```python
import jax
import jax.numpy as jnp
from jax import lax
from jax.experimental import pallas as pl
from jax.experimental.pallas import tpu as pltpu
from jax.sharding import PartitionSpec as P

BETA_ONE = 0.9
BETA_TWO = 0.999
EPS_ADAM = 1e-08
RATE = 0.3
DECAY = 0.1
EPS_NORM = 1e-05
OUTER_RATE = 0.7
MOMENTUM = 0.9
MIXING = 0.5

INNER = 2
NX = 4
NZ = 4
NF = NX * NZ
TOK = 128
ROWS = 256
HALF = ROWS // 2
D = ROWS * NF
KW = 512
NP = 8
NL = 4
PART = ROWS // NP
SUB = PART // NL
PARTS = (4, 1)
ORDER = (2, 1, 3, 0)

FAR_FIRST = [(j, i) for j in (2, 1, 3, 0) for i in (2, 1, 3, 0) if i + j > 0]

MESH = pl.DeviceIdType.MESH


def flip(value, bits):
    if bits == 0:
        return value
    if bits == 1:
        return value + 1 - 2 * (value % 2)
    if bits == 2:
        return (value + 2) % 4
    return 3 - value


def adam_update(current, gradient, moment_one, moment_two, decay_rate):
    moment_one = BETA_ONE * moment_one + (1.0 - BETA_ONE) * gradient
    moment_two = BETA_TWO * moment_two + (1.0 - BETA_TWO) * gradient * gradient
    current = current - RATE * (
        moment_one / (jnp.sqrt(moment_two) + EPS_ADAM) + decay_rate * current
    )
    return (current, moment_one, moment_two)


def outer_step(anchor, momentum, mean_delta):
    velocity = MOMENTUM * momentum + mean_delta
    return anchor - OUTER_RATE * (mean_delta + MOMENTUM * velocity)


def kernel(
    inputs,
    cotangent,
    weight,
    adam_first,
    adam_second,
    anchor_weight,
    outer_weight,
    norm_gain,
    gain_first,
    gain_second,
    anchor_gain,
    outer_gain,
    out_weight,
    out_gain,
    xin,
    cin,
    win,
    m_one,
    m_two,
    columns,
    scaled,
    grads,
    keep,
    z_out,
    z_in,
    norms,
    parts,
    part_sum,
    subs,
    merged,
    anchor_rows,
    outer_rows,
    gain_in,
    gains,
    gain_parts,
    gain_subs,
    local_sem,
    x_send,
    x_recv,
    c_send,
    c_recv,
    z_send,
    z_recv,
    q_send,
    q_recv,
    p_send,
    p_recv,
    l_send,
    l_recv,
):
    replicas = NP * NL
    rep = lax.axis_index("rep")
    my_part = rep % NP
    my_plane = rep // NP
    me = lax.axis_index("fsdp")
    my_z = me // NX
    my_x = me % NX

    def at(z, x):
        return {"fsdp": z * NX + x}

    def in_plane(k):
        return {"rep": my_plane * NP + (my_part + k) % NP}

    def over_planes(k):
        return {"rep": (my_plane + k) % NL * NP + my_part}

    barrier = pltpu.get_barrier_semaphore()
    for j, i in ((0, 1), (0, 3), (0, 2), (1, 0), (3, 0)):
        pl.semaphore_signal(
            barrier, inc=1, device_id=at(flip(my_z, j), flip(my_x, i)), device_id_type=MESH
        )
    for k in range(1, NP):
        pl.semaphore_signal(barrier, inc=1, device_id=in_plane(k), device_id_type=MESH)
    for k in range(1, NL):
        pl.semaphore_signal(barrier, inc=1, device_id=over_planes(k), device_id_type=MESH)

    def part_of(part):
        return pl.ds(pl.multiple_of(part * PART, PART), PART)

    sub_rows = pl.ds(pl.multiple_of(my_part * PART + my_plane * SUB, SUB), SUB)

    loads = []
    for place, (source, target) in enumerate(
        (
            (inputs.at[0], xin.at[0]),
            (cotangent, cin),
            (inputs.at[1], xin.at[1]),
            (weight, win),
            (adam_first, m_one),
            (adam_second, m_two),
            (anchor_weight.at[sub_rows], anchor_rows),
            (outer_weight.at[sub_rows], outer_rows),
            (norm_gain, gain_in.at[0]),
            (gain_first, gain_in.at[1]),
            (gain_second, gain_in.at[2]),
            (anchor_gain, gain_in.at[3]),
            (outer_gain, gain_in.at[4]),
        )
    ):
        copy = pltpu.make_async_copy(source, target, local_sem.at[place])
        copy.start()
        loads.append(copy)

    def column(j, i):
        owner = flip(my_z, j) * NX + flip(my_x, i)
        return pl.ds(pl.multiple_of(owner * ROWS, ROWS), ROWS)

    own_copies = {}
    place = len(loads)
    for s in range(INNER):
        for j in ORDER:
            copy = pltpu.make_async_copy(
                inputs.at[s, :, column(j, 0)],
                columns.at[s, j, pl.ds(0, TOK)],
                local_sem.at[place],
            )
            copy.start()
            own_copies[s, j] = copy
            place += 1

    sends = []

    def send(source, target, send_sem, recv_sem, device):
        copy = pltpu.make_async_remote_copy(
            src_ref=source,
            dst_ref=target,
            send_sem=send_sem,
            recv_sem=recv_sem,
            device_id=device,
            device_id_type=MESH,
        )
        copy.start()
        sends.append(copy)
        return copy

    x_copies = {}
    c_copies = {}
    z_copies = {}
    q_copies = {}

    def send_columns(s, j):
        x_copies[s, j] = [
            send(
                inputs.at[s, :, column(j, i)],
                columns.at[s, j, pl.ds(i * TOK, TOK)],
                x_send.at[s, j, i - 1],
                x_recv.at[s, j, i - 1],
                at(my_z, flip(my_x, i)),
            )
            for i in (1, 3, 2)
        ]

    def scale(s):
        values = xin[s].astype(jnp.float32)
        mean = jnp.mean(values * values, axis=-1, keepdims=True)
        scale = lax.rsqrt(mean + EPS_NORM)
        scaled[s, pl.ds(0, TOK), :] = (cin[s].astype(jnp.float32) * scale).astype(
            jnp.bfloat16
        )

    def send_scaled(s, part, width):
        columns_of = pl.ds(part * width, width)
        c_copies[s, part] = [
            send(
                scaled.at[s, pl.ds(0, TOK), columns_of],
                scaled.at[s, pl.ds(i * TOK, TOK), columns_of],
                c_send.at[s, part, i - 1],
                c_recv.at[s, part, i - 1],
                at(my_z, flip(my_x, i)),
            )
            for i in (1, 3, 2)
        ]

    def send_rows(s, slot, j, part=0, width=KW):
        columns_of = pl.ds(part * width, width)
        sem = slot if part == 0 else 4 + 2 * part + slot
        z_copies[s, sem] = send(
            z_out.at[s, slot, :, columns_of],
            z_in.at[s, slot, :, columns_of],
            z_send.at[s, sem],
            z_recv.at[s, sem],
            at(flip(my_z, j), my_x),
        )

    def sent(s, *slots):
        for slot in slots:
            copy = z_copies[s, slot]
            copy.wait_send()
            sends[:] = [other for other in sends if other is not copy]


    def exchange(stage, sems, count, source, target, device):
        return [
            send(
                source(k),
                target(k),
                sems[0].at[stage, k - 1],
                sems[1].at[stage, k - 1],
                device(k),
            )
            for k in range(1, count)
        ]

    planes = (p_send, p_recv), NP
    levels = (l_send, l_recv), NL

    def rep_start():
        return exchange(
            0,
            *planes,
            lambda k: weight.at[part_of((my_part + k) % NP)],
            lambda k: parts.at[k],
            in_plane,
        ) + exchange(
            1, *planes, lambda k: gain_in.at[0], lambda k: gain_parts.at[k], in_plane
        )

    def rep_second(copies):
        for copy in copies:
            copy.wait_recv()
        loads[3].wait()
        total = win[part_of(my_part), :]
        for k in range(1, NP):
            total = total + parts[k]
        part_sum[...] = total
        gain_total = gain_in[0]
        for k in range(1, NP):
            gain_total = gain_total + gain_parts[k]
        gain_subs[0] = gain_total
        return exchange(
            0,
            *levels,
            lambda k: part_sum.at[
                pl.ds(pl.multiple_of((my_plane + k) % NL * SUB, SUB), SUB)
            ],
            lambda k: subs.at[k],
            over_planes,
        ) + exchange(
            1, *levels, lambda k: gain_subs.at[0], lambda k: gain_subs.at[k], over_planes
        )

    def rep_third(copies):
        for copy in copies:
            copy.wait_recv()
        total = part_sum[pl.ds(pl.multiple_of(my_plane * SUB, SUB), SUB), :]
        for k in range(1, NL):
            total = total + subs[k]
        loads[6].wait()
        loads[7].wait()
        anchor = anchor_rows[...]
        merged[sub_rows, :] = outer_step(
            anchor, outer_rows[...], anchor - total / replicas
        )
        return exchange(
            2,
            *levels,
            lambda k: merged.at[sub_rows],
            lambda k: merged.at[sub_rows],
            over_planes,
        )

    def rep_fourth(copies):
        for copy in copies:
            copy.wait_recv()
        return exchange(
            2,
            *planes,
            lambda k: merged.at[part_of(my_part)],
            lambda k: merged.at[part_of(my_part)],
            in_plane,
        )

    low = pl.ds(0, HALF)
    high = pl.ds(HALF, HALF)

    def multiply(s, j, columns_of):
        return lax.dot_general(
            columns[s, j],
            scaled[s, :, columns_of],
            (((0,), (0,)), ((), ())),
            preferred_element_type=jnp.float32,
        )

    def arrived(s, j, part=None):
        if part in (None, 0):
            own_copies[s, j].wait()
            for copy in x_copies[s, j]:
                copy.wait_recv()
        if part is not None:
            for copy in c_copies[s, part]:
                copy.wait_recv()

    def first_product(s, parts_of):
        width = KW // parts_of
        for part in range(parts_of):
            arrived(s, 2, part)
            columns_of = pl.ds(part * width, width)
            block = multiply(s, 2, columns_of)
            z_out[s, 0, :, columns_of] = block[:HALF].astype(jnp.bfloat16)
            z_out[s, 1, :, columns_of] = block[HALF:].astype(jnp.bfloat16)
            if s == 0:
                send_rows(s, 0, 1, part, width)
                send_rows(s, 1, 3, part, width)

    def product(s, j):
        arrived(s, j)
        block = multiply(s, j, pl.ds(0, KW))
        if j == 1:
            z_out[s, 2] = block[:HALF].astype(jnp.bfloat16)
            keep[s, 1] = block[HALF:]
        elif j == 3:
            z_out[s, 3] = block[HALF:].astype(jnp.bfloat16)
            keep[s, 0] = block[:HALF]
        else:
            grads[s] = block

    def forward(s):
        for slot, target, j in ((0, 4, 3), (1, 5, 1)):
            z_copies[s, slot].wait_recv()
            for part in range(1, PARTS[s]):
                z_copies[s, 4 + 2 * part + slot].wait_recv()
            total = keep[s, slot] + z_in[s, slot].astype(jnp.float32)
            z_out[s, target] = total.astype(jnp.bfloat16)
            send_rows(s, target, j)

    def reduce_rows(s):
        for slot in (2, 3, 4, 5):
            z_copies[s, slot].wait_recv()
        grads[s, low] = grads[s, low] + (
            z_in[s, 2].astype(jnp.float32) + z_in[s, 4].astype(jnp.float32)
        )
        grads[s, high] = grads[s, high] + (
            z_in[s, 3].astype(jnp.float32) + z_in[s, 5].astype(jnp.float32)
        )

    def send_norm(s, current, gain):
        product_sum = grads[s]
        low_weight = current.astype(jnp.bfloat16).astype(jnp.float32)
        grad_gain = jnp.sum(product_sum * low_weight, axis=1, keepdims=True)
        grad_weight = product_sum * gain
        squares = grad_weight * grad_weight
        folded = squares[:, 0:128] + squares[:, 128:256] + squares[:, 256:384] + squares[:, 384:512]
        lane = lax.broadcasted_iota(jnp.int32, (ROWS, 128), 1)
        folded = folded + jnp.where(lane == 0, grad_gain * grad_gain, 0.0)
        norms[s, 0] = jnp.sum(folded, axis=0, keepdims=True)
        q_copies[s] = [
            send(
                norms.at[s, 0],
                norms.at[s, k],
                q_send.at[s, k - 1],
                q_recv.at[s, k - 1],
                at(flip(my_z, j), flip(my_x, i)),
            )
            for k, (j, i) in enumerate(FAR_FIRST, 1)
        ]
        return grad_gain

    def update(s, current, gain, grad_gain, moments, gain_moments):
        for copy in q_copies[s]:
            copy.wait_recv()
        total = jnp.sum(jnp.sum(norms[s], axis=0), keepdims=True)
        factor = jnp.minimum(1.0, 1.0 / (jnp.sqrt(total) + 1e-06))
        current, one, two = adam_update(
            current, factor * (grads[s] * gain), moments[0], moments[1], DECAY
        )
        gain, gain_one, gain_two = adam_update(
            gain, factor * grad_gain, gain_moments[0], gain_moments[1], 0.0
        )
        return current, gain, (one, two), (gain_one, gain_two)

    pl.semaphore_wait(barrier, 5 + NP + NL - 2)

    send_columns(0, 2)
    for copy in loads[:2]:
        copy.wait()
    scale(0)
    for part in range(PARTS[0]):
        send_scaled(0, part, KW // PARTS[0])
    for copy in loads[8:]:
        copy.wait()
    gains[...] = jnp.concatenate(
        [gain_in[k] for k in range(5)] + [jnp.zeros((3, ROWS), jnp.float32)], axis=0
    )
    rep_copies = rep_start()
    send_columns(0, 1)
    first_product(0, PARTS[0])
    send_columns(0, 3)
    send_columns(0, 0)
    product(0, 1)
    send_rows(0, 2, 1)
    loads[2].wait()
    scale(1)
    send_scaled(1, 0, KW)
    send_columns(1, 2)
    product(0, 3)
    send_rows(0, 3, 3)
    product(0, 0)
    send_columns(1, 1)
    send_columns(1, 3)
    send_columns(1, 0)
    rep_copies = rep_second(rep_copies)
    forward(0)
    first_product(1, 1)
    sent(0, 2, 3)
    send_rows(1, 0, 1)
    send_rows(1, 1, 3)
    rep_copies = rep_third(rep_copies)
    product(1, 1)
    product(1, 3)
    product(1, 0)
    for copy in loads[4:6]:
        copy.wait()
    turned = jnp.transpose(gains[...])
    current, gain = win[...], turned[:, 0:1]
    sent(0, 4, 5)
    reduce_rows(0)
    grad_gain = send_norm(0, current, gain)
    send_rows(1, 2, 1)
    send_rows(1, 3, 3)
    forward(1)
    rep_copies = rep_fourth(rep_copies)
    current, gain, moments, gain_moments = update(
        0,
        current,
        gain,
        grad_gain,
        (m_one[...].astype(jnp.float32), m_two[...].astype(jnp.float32)),
        (turned[:, 1:2], turned[:, 2:3]),
    )
    for copy in rep_copies:
        copy.wait_recv()
    for copy in sends:
        copy.wait_send()
    sends.clear()
    reduce_rows(1)
    grad_gain = send_norm(1, current, gain)
    current, gain, _, _ = update(1, current, gain, grad_gain, moments, gain_moments)
    out_weight[...] = MIXING * current + (1.0 - MIXING) * merged[...]
    gain_total = gain_subs[0]
    for k in range(1, NL):
        gain_total = gain_total + gain_subs[k]
    anchor_row = gains[3:4, :]
    new_gain = outer_step(
        anchor_row, gains[4:5, :], anchor_row - gain_total / replicas
    )
    gain_row = jnp.transpose(jnp.broadcast_to(gain, (ROWS, 8)))
    out_gain[...] = MIXING * gain_row[0:1, :] + (1.0 - MIXING) * new_gain
    for copy in sends:
        copy.wait_send()


def window(*operands):
    anywhere = pl.BlockSpec(memory_space=pl.ANY)
    vmem = pl.BlockSpec(memory_space=pltpu.VMEM)
    dma = pltpu.SemaphoreType.DMA
    f32, bf16 = jnp.float32, jnp.bfloat16
    return pl.pallas_call(
        kernel,
        out_shape=(
            jax.ShapeDtypeStruct((ROWS, KW), f32),
            jax.ShapeDtypeStruct((1, ROWS), f32),
        ),
        in_specs=[anywhere] * len(operands),
        out_specs=(vmem, vmem),
        scratch_shapes=[
            pltpu.VMEM((INNER, TOK, D), bf16),
            pltpu.VMEM((INNER, TOK, KW), bf16),
            pltpu.VMEM((ROWS, KW), f32),
            pltpu.VMEM((ROWS, KW), bf16),
            pltpu.VMEM((ROWS, KW), bf16),
            pltpu.VMEM((INNER, NZ, NX * TOK, ROWS), bf16),
            pltpu.VMEM((INNER, NX * TOK, KW), bf16),
            pltpu.VMEM((INNER, ROWS, KW), f32),
            pltpu.VMEM((INNER, 2, HALF, KW), f32),
            pltpu.VMEM((INNER, 6, HALF, KW), bf16),
            pltpu.VMEM((INNER, 6, HALF, KW), bf16),
            pltpu.VMEM((INNER, NF, 1, 128), f32),
            pltpu.VMEM((NP, PART, KW), f32),
            pltpu.VMEM((PART, KW), f32),
            pltpu.VMEM((NL, SUB, KW), f32),
            pltpu.VMEM((ROWS, KW), f32),
            pltpu.VMEM((SUB, KW), f32),
            pltpu.VMEM((SUB, KW), f32),
            pltpu.VMEM((5, 1, ROWS), f32),
            pltpu.VMEM((8, ROWS), f32),
            pltpu.VMEM((NP, 1, ROWS), f32),
            pltpu.VMEM((NL, 1, ROWS), f32),
            dma((13 + INNER * NZ,)),
            dma((INNER, NZ, NX - 1)),
            dma((INNER, NZ, NX - 1)),
            dma((INNER, PARTS[0], NX - 1)),
            dma((INNER, PARTS[0], NX - 1)),
            dma((INNER, 4 + 2 * PARTS[0])),
            dma((INNER, 4 + 2 * PARTS[0])),
            dma((INNER, NF - 1)),
            dma((INNER, NF - 1)),
            dma((3, NP - 1)),
            dma((3, NP - 1)),
            dma((3, NL - 1)),
            dma((3, NL - 1)),
        ],
        compiler_params=pltpu.CompilerParams(
            collective_id=0, has_side_effects=True, vmem_limit_bytes=60 * 1024 * 1024
        ),
        cost_estimate=pl.CostEstimate(
            flops=4 * INNER * NX * TOK * NZ * ROWS * KW,
            bytes_accessed=8 * 1024 * 1024,
            transcendentals=0,
        ),
        name="inner_window",
    )(*operands)


def on_device(
    inputs,
    cotangent,
    weight,
    norm_gain,
    adam_first,
    adam_second,
    gain_first,
    gain_second,
    anchor_weight,
    anchor_gain,
    outer_weight,
    outer_gain,
):
    merged_weight, merged_gain = window(
        inputs,
        cotangent,
        weight[0],
        adam_first[0],
        adam_second[0],
        anchor_weight,
        outer_weight,
        norm_gain,
        gain_first,
        gain_second,
        anchor_gain[None],
        outer_gain[None],
    )
    return (merged_weight[None], merged_gain)


def solution(mesh):
    return jax.shard_map(
        on_device,
        mesh=mesh,
        in_specs=(
            P(None, ("rep", "fsdp"), None),
            P(None, ("rep", "fsdp"), None),
            P("rep", "fsdp", None),
            P("rep", "fsdp"),
            P("rep", "fsdp", None),
            P("rep", "fsdp", None),
            P("rep", "fsdp"),
            P("rep", "fsdp"),
            P("fsdp", None),
            P("fsdp"),
            P("fsdp", None),
            P("fsdp"),
        ),
        out_specs=(P("rep", "fsdp", None), P("rep", "fsdp")),
        check_vma=False,
    )
```
